32 devices in a mesh: site: 4 (over z), fault: 8 (over y, x, core).
Axes of the slice: x: 2, y: 2, z: 4, core: 2. Of those that a mesh axis runs over, the one named last changes fastest.
Arguments:
- green_tensor: bfloat16 [4, 128, 96, 6, 256], P('site', 'fault'), may hold values from -0.375 to 0.375
- slip_map: bfloat16 [128, 8, 256], P('fault', None, 'site'), may hold values from 0.19921875 to 2
- rupture_time: float32 [128, 8, 256], P('fault', None, 'site'), may hold values from 0 to 48
- variation_ids: int32 [128, 8], P('fault'), may hold values from 0 to 7, each once within a row
- variation_count: int32 [128], P('fault'), may hold values from 2 to 8, as said below
- tile_rupture: int32 [128], P('fault'), may hold values from 0 to 7
- owner_slot: int32 [8], replicated, may hold values from 0 to 7, each once
Outputs:
- seismograms: float32 [8, 8, 4, 3, 192], P('fault', None, 'site')
The draws below stay inside these ranges and needn't reach their ends.
Inputs may be any that keep to these rules, and one draw needn't show every extreme that they name: `variation_count`: every tile lists at least 2 of the 8 variations, and in every draw some tile lists all 8.
All inputs are finite; a program needn't handle non-finite values.
Results may differ from the reference program's by a relative error of at most 0.0027.
Values sent between devices are 32-bit elements; how exact they have to be, the bound alone decides.
A program may use at most 64 MiB of HBM per device.

```python
import math
import jax
import jax.numpy as jnp
from jax import lax

P_SIZE = 256
F = 96
C = 3
VMAX = 8
NT = 192
SITES = 4
TILES = 128
RUPT = 8


def draw_variation_count(key, part):
    first_key, second_key = jax.random.split(jax.random.fold_in(key, 7))
    counts = jax.random.randint(first_key, (TILES,), VMAX // 3, VMAX + 1)
    full_tile = jax.random.randint(second_key, (), 0, TILES)
    return counts.at[full_tile].set(VMAX).astype(jnp.int32)


def place_ends(entries, rng, smallest, top_value):
    longest = entries.shape.index(max(entries.shape))
    spots = []
    for shift in (0, 1):
        where = [jax.random.randint(jax.random.fold_in(rng, axis), (), 0, length) for axis, length in enumerate(entries.shape)]
        where[longest] = (where[longest] + shift) % entries.shape[longest]
        spots.append(tuple(where))
    return entries.at[spots[0]].set(smallest).at[spots[1]].set(top_value)


def block_levels(stream_key, shape, cuts, smallest, high):
    level, own = 1.0, jax.random.fold_in(stream_key, 6)
    for axis_at, blocks in cuts:
        draws = jnp.exp(jax.random.uniform(jax.random.fold_in(own, axis_at), (blocks,), jnp.float32, smallest / len(cuts), high / len(cuts)))
        level = level * jnp.repeat(draws, shape[axis_at] // blocks).reshape([-1 if axis == axis_at else 1 for axis in range(len(shape))])
    return level


def scatter_about(own_key, dims, spread, most, cuts=(), kind=jnp.bfloat16):
    factor_of = block_levels(own_key, dims, cuts, -0.22, 0.18) if cuts else 1.0
    result = jax.random.normal(own_key, dims, jnp.float32) * spread * factor_of
    return jnp.minimum(jnp.maximum(result, -most), most).astype(kind)


def setup_inputs(seed: int = 0) -> dict:
    arg_keys = jax.random.split(jax.random.key(seed), 8)
    green_tensor = scatter_about(arg_keys[0], (SITES, TILES, F, 2 * C, P_SIZE), P_SIZE ** -0.5, 0.375, ((0, 4), (1, 8)))
    slip_map = jnp.clip(jnp.exp(math.log(2.0) - 2.306499 * jax.random.uniform(arg_keys[1], (TILES, VMAX, P_SIZE), jnp.float32) ** block_levels(arg_keys[1], (TILES, VMAX, P_SIZE), ((0, 8), (2, 4)), -0.2, 0.2)), 0.19921875, 2.0).astype(jnp.bfloat16)
    rupture_time = jnp.clip(48.0 * jax.random.uniform(arg_keys[2], (TILES, VMAX, P_SIZE), jnp.float32) ** block_levels(arg_keys[2], (TILES, VMAX, P_SIZE), ((0, 8), (2, 4)), -0.2, 0.2), 0.0, 48.0)
    variation_ids = jax.vmap(lambda own: jax.random.permutation(own, VMAX))(jax.random.split(arg_keys[3], TILES)).reshape((TILES, VMAX)).astype(jnp.int32)
    variation_count = draw_variation_count(jax.random.fold_in(arg_keys[7], 71), 0)
    tile_rupture = place_ends(jax.random.randint(arg_keys[5], (TILES,), 0, RUPT), jax.random.fold_in(arg_keys[5], 1), 0, RUPT - 1).astype(jnp.int32)
    owner_slot = jax.random.permutation(arg_keys[6], RUPT).astype(jnp.int32)
    return {"green_tensor": green_tensor, "slip_map": slip_map, "rupture_time": rupture_time, "variation_ids": variation_ids, "variation_count": variation_count, "tile_rupture": tile_rupture, "owner_slot": owner_slot}


def inverse_table(freq_count):
    sample_count = 2 * freq_count
    wave = jnp.arange(freq_count, dtype=jnp.int32)[:, None]
    sample = jnp.arange(sample_count, dtype=jnp.int32)[None, :]
    angles = 2.0 * math.pi / sample_count * (wave * sample % sample_count).astype(jnp.float32)
    return jnp.concatenate([jnp.cos(angles), -jnp.sin(angles)], axis=0) / math.sqrt(freq_count)

def reference(green_tensor, slip_map, rupture_time, variation_ids, variation_count, tile_rupture, owner_slot):
    frequency = jnp.arange(F, dtype=jnp.float32)
    tile_total = slip_map.shape[0]
    initial = jnp.zeros((RUPT, VMAX, SITES, C, 2 * F), jnp.float32)

    def one_tile(tile_index, accumulated):
        green_tile = lax.dynamic_index_in_dim(green_tensor, tile_index, 1, keepdims=False).astype(jnp.float32)
        amplitude = slip_map[tile_index].astype(jnp.float32)
        arrival = rupture_time[tile_index]
        phases = 2.0 * math.pi / NT * frequency[:, None, None] * arrival[None]
        a_real = lax.optimization_barrier((amplitude[None] * jnp.cos(phases)).astype(jnp.bfloat16)).astype(jnp.float32)
        a_imag = lax.optimization_barrier((-amplitude[None] * jnp.sin(phases)).astype(jnp.bfloat16)).astype(jnp.float32)
        part_real = jnp.einsum('fvp,sfkp->vskf', a_real, green_tile, precision=lax.Precision.HIGHEST)
        part_imag = jnp.einsum('fvp,sfkp->vskf', a_imag, green_tile, precision=lax.Precision.HIGHEST)
        real_part = part_real[:, :, :C] - part_imag[:, :, C:]
        imag_part = part_real[:, :, C:] + part_imag[:, :, :C]
        spectrum = jnp.concatenate([real_part, imag_part], axis=-1)
        is_live = (jnp.arange(VMAX, dtype=jnp.int32) < variation_count[tile_index]).astype(jnp.float32)
        spectrum = spectrum * is_live[:, None, None, None]
        return accumulated.at[tile_rupture[tile_index], variation_ids[tile_index]].add(spectrum)
    accumulated = lax.fori_loop(0, tile_total, one_tile, initial)
    table = inverse_table(F)
    seismic = jnp.dot(accumulated.reshape(-1, 2 * F), table, precision=lax.Precision.HIGHEST, preferred_element_type=jnp.float32)
    seismic = seismic.reshape(RUPT, VMAX, SITES, C, NT)
    return jnp.zeros_like(seismic).at[owner_slot].set(seismic)
```

```python
import functools
import math

import jax
import jax.numpy as jnp
from jax import lax
from jax.experimental import pallas as pl
from jax.experimental.pallas import tpu as pltpu
from jax.sharding import PartitionSpec as P

BLOCK = 32
HALF = 8


def inverse_table(freq_count):
    sample_count = 2 * freq_count
    wave = jnp.arange(freq_count, dtype=jnp.int32)[:, None]
    sample = jnp.arange(sample_count, dtype=jnp.int32)[None, :]
    angles = 2.0 * math.pi / sample_count * (wave * sample % sample_count).astype(jnp.float32)
    return jnp.concatenate([jnp.cos(angles), -jnp.sin(angles)], axis=0) / math.sqrt(freq_count)


def cos_sin(angle):
    x = angle - math.pi / 4
    y = x * x
    c = jnp.float32(1.0)
    s = jnp.float32(1.0)
    for n in (5, 4, 3, 2, 1):
        c = 1.0 - y * (c * (1.0 / ((2 * n - 1) * (2 * n))))
        s = 1.0 - y * (s * (1.0 / ((2 * n) * (2 * n + 1))))
    s = s * x
    root = math.sqrt(0.5)
    return root * (c - s), root * (c + s)


def turn(a, b):
    return a[0] * b[0] - a[1] * b[1], a[0] * b[1] + a[1] * b[0]


def phasor_blocks(amplitude, arrival, freq_count, write):
    one = cos_sin(arrival * (2.0 * math.pi / (2 * freq_count)))
    one = (one[0], -one[1])
    powers = [None, one]
    for n in range(2, HALF + 1):
        powers.append(turn(powers[n // 2], powers[n - n // 2]))
    step = turn(powers[HALF], powers[HALF])
    centre = (amplitude * powers[HALF][0], amplitude * powers[HALF][1])
    for k in range(HALF, freq_count, 2 * HALF):
        write(k, *centre)
        for n in range(1, HALF + 1):
            cc, ss = centre[0] * powers[n][0], centre[1] * powers[n][1]
            cs, sc = centre[0] * powers[n][1], centre[1] * powers[n][0]
            write(k - n, cc + ss, sc - cs)
            if n < HALF:
                write(k + n, cc - ss, sc + cs)
        if k + 2 * HALF < freq_count:
            centre = turn(centre, step)


def compute_tile(tile, amplitude, arrival, green, phasor, spectrum):
    rows, points = amplitude.shape
    freq_count = green.shape[2]
    lanes = 4 * BLOCK
    for start in range(0, points, lanes):
        piece = slice(start, start + lanes)

        def write(k, real, imag):
            both = jnp.concatenate([real, imag], axis=0).astype(jnp.bfloat16)
            phasor[k * 2 * rows : (k + 1) * 2 * rows, piece] = both

        phasor_blocks(amplitude[:, piece], arrival[:, piece], freq_count, write)
    lane = lax.broadcasted_iota(jnp.int32, (2 * rows, 2 * lanes), 1) % BLOCK
    for block in range(freq_count // BLOCK):
        own = pl.ds(block * BLOCK, BLOCK)
        weights = jnp.concatenate([green[tile, c, own, :] for c in (0, 1, 2, 2, 3, 4, 5, 5)], axis=0)
        left = phasor[block * BLOCK * 2 * rows : (block + 1) * BLOCK * 2 * rows, :]
        product = lax.dot_general(
            left, weights, (((1,), (1,)), ((), ())), preferred_element_type=jnp.float32
        )
        picked = product[: 2 * rows]
        for k in range(1, BLOCK):
            picked = jnp.where(lane == k, product[k * 2 * rows : (k + 1) * 2 * rows], picked)
        real = picked[:rows, :lanes] - picked[rows:, lanes:]
        imag = picked[:rows, lanes:] + picked[rows:, :lanes]
        target = pl.ds(pl.multiple_of(tile * rows, rows), rows)
        spectrum[target, pl.ds(2 * block * lanes, lanes)] = real
        spectrum[target, pl.ds((2 * block + 1) * lanes, lanes)] = imag


def route_rows(ids, count, rupture, owner, spectrum, row_count, rupture_total):
    tile_total = ids.shape[1]
    wide = row_count * rupture_total
    column = lax.broadcasted_iota(jnp.int32, (row_count, wide), 1)
    slot = lax.broadcasted_iota(jnp.int32, (row_count, 1), 0)
    pieces = []
    for tile in range(tile_total):
        place = owner[rupture[tile]] * row_count
        target = jnp.where(slot < count[tile], ids[:, tile : tile + 1] + place, -1)
        pieces.append((column == target).astype(jnp.float32))
    member = jnp.concatenate(pieces, axis=0).astype(jnp.bfloat16)
    value = spectrum[...]
    high = value.astype(jnp.bfloat16)
    low = (value - high.astype(jnp.float32)).astype(jnp.bfloat16)
    dims = (((0,), (0,)), ((), ()))
    return lax.dot_general(
        jnp.concatenate([member, member], axis=0),
        jnp.concatenate([high, low], axis=0),
        dims,
        preferred_element_type=jnp.float32,
    )


def kernel(ids, count, rupture, owner, amplitude, arrival, green_hbm, out, green, phasor, spectrum, sems):
    tile_total, rows, _ = amplitude.shape
    for tile in range(tile_total):
        pltpu.make_async_copy(green_hbm.at[tile], green.at[tile], sems.at[tile]).start()

    def one(tile, carry):
        pltpu.make_async_copy(green_hbm.at[tile], green.at[tile], sems.at[tile]).wait()
        compute_tile(tile, amplitude[tile], arrival[tile], green, phasor, spectrum)
        return carry

    lax.fori_loop(0, tile_total, one, 0)
    out[...] = route_rows(ids, count, rupture, owner, spectrum, rows, owner.shape[0])


def per_device(
    green_tensor, slip_map, rupture_time, variation_ids, variation_count, tile_rupture, owner_slot
):
    green = jnp.swapaxes(green_tensor[0], 1, 2)
    tile_total, _, freq_count, points = green.shape
    rows = slip_map.shape[1]
    rupture_total = owner_slot.shape[0]
    local = jnp.concatenate([slip_map.astype(jnp.float32), rupture_time], axis=1)
    maps = lax.all_gather(local, "site", axis=2, tiled=True)
    width = 8 * freq_count
    smem = pl.BlockSpec(memory_space=pltpu.SMEM)
    vmem = pl.BlockSpec(memory_space=pltpu.VMEM)
    local_sum = pl.pallas_call(
        kernel,
        out_shape=jax.ShapeDtypeStruct((rupture_total * rows, width), jnp.float32),
        in_specs=[vmem, smem, smem, smem, vmem, vmem, pl.BlockSpec(memory_space=pl.ANY)],
        out_specs=vmem,
        scratch_shapes=[
            pltpu.VMEM(green.shape, jnp.bfloat16),
            pltpu.VMEM((freq_count * 2 * rows, points), jnp.bfloat16),
            pltpu.VMEM((tile_total * rows, width), jnp.float32),
            pltpu.SemaphoreType.DMA((tile_total,)),
        ],
        compiler_params=pltpu.CompilerParams(vmem_limit_bytes=40 * 1024 * 1024),
        cost_estimate=pl.CostEstimate(flops=2 * 10**9, bytes_accessed=5 * 10**6, transcendentals=0),
    )(
        variation_ids.T, variation_count, tile_rupture, owner_slot,
        maps[:, :rows], maps[:, rows:], green,
    )
    blocks = freq_count // BLOCK
    packed = local_sum.reshape(rupture_total, rows, blocks, 2, 4, BLOCK)[:, :, :, :, :3]
    packed = packed.reshape(rupture_total, -1)
    received = lax.all_to_all(packed, "fault", split_axis=0, concat_axis=0, tiled=True)
    devices = lax.axis_size("fault")
    owned = jnp.sum(received.reshape(devices, rupture_total // devices, -1), axis=0)
    owned = owned.reshape(-1, rows, blocks, 2, 3, BLOCK)
    owned = owned.transpose(0, 1, 4, 3, 2, 5).reshape(-1, 2 * freq_count)
    seismic = jnp.dot(
        owned,
        inverse_table(freq_count),
        precision=lax.Precision.HIGHEST,
        preferred_element_type=jnp.float32,
    )
    return seismic.reshape(rupture_total // devices, rows, 1, 3, 2 * freq_count)


def solution(mesh):
    placed = (
        P("site", "fault", None, None, None),
        P("fault", None, "site"),
        P("fault", None, "site"),
        P("fault", None),
        P("fault"),
        P("fault"),
        P(),
    )
    return jax.shard_map(
        per_device,
        mesh=mesh,
        in_specs=placed,
        out_specs=P("fault", None, "site", None, None),
        check_vma=False,
    )
```

```python
import functools
import math

import jax
import jax.numpy as jnp
import numpy as np
from jax import lax
from jax.experimental import pallas as pl
from jax.experimental.pallas import tpu as pltpu
from jax.sharding import PartitionSpec as P

BLOCK = 32
HALF = 8
CHUNKS = 4
UNROLL = 2
MESH = pl.DeviceIdType.MESH


def inverse_table(freq_count):
    sample_count = 2 * freq_count
    wave = np.arange(freq_count)[:, None]
    sample = np.arange(sample_count)[None, :]
    angles = 2.0 * math.pi / sample_count * (wave * sample % sample_count)
    table = np.concatenate([np.cos(angles), -np.sin(angles)], axis=0) / math.sqrt(freq_count)
    return table.astype(np.float32)


def cos_sin(angle):
    x = angle - math.pi / 4
    y = x * x
    c = jnp.float32(1.0)
    s = jnp.float32(1.0)
    for n in (5, 4, 3, 2, 1):
        c = 1.0 - y * (c * (1.0 / ((2 * n - 1) * (2 * n))))
        s = 1.0 - y * (s * (1.0 / ((2 * n) * (2 * n + 1))))
    s = s * x
    root = math.sqrt(0.5)
    return root * (c - s), root * (c + s)


def turn(a, b):
    return a[0] * b[0] - a[1] * b[1], a[0] * b[1] + a[1] * b[0]


def phasor_blocks(pieces, freq_count, write):
    tables, steps, centres = [], [], []
    for amplitude, arrival in pieces:
        one = cos_sin(arrival * (2.0 * math.pi / (2 * freq_count)))
        one = (one[0], -one[1])
        powers = [None, one]
        for n in range(2, HALF + 1):
            powers.append(turn(powers[n // 2], powers[n - n // 2]))
        tables.append(powers)
        steps.append(turn(powers[HALF], powers[HALF]))
        centres.append((amplitude * powers[HALF][0], amplitude * powers[HALF][1]))
    for k in range(HALF, freq_count, 2 * HALF):
        for piece, powers in enumerate(tables):
            centre = centres[piece]
            write(k, piece, *centre)
            for n in range(1, HALF + 1):
                cc, ss = centre[0] * powers[n][0], centre[1] * powers[n][1]
                cs, sc = centre[0] * powers[n][1], centre[1] * powers[n][0]
                write(k - n, piece, cc + ss, sc - cs)
                if n < HALF:
                    write(k + n, piece, cc - ss, sc + cs)
            if k + 2 * HALF < freq_count:
                centres[piece] = turn(centre, steps[piece])


def make_phasors(amplitude, arrival, freq_count, phasor):
    rows, points = amplitude.shape
    lanes = 4 * BLOCK

    def write(k, piece, real, imag):
        both = jnp.concatenate([real, imag], axis=0).astype(jnp.bfloat16)
        phasor[k * 2 * rows : (k + 1) * 2 * rows, piece * lanes : (piece + 1) * lanes] = both

    cuts = [slice(at, at + lanes) for at in range(0, points, lanes)]
    phasor_blocks([(amplitude[:, cut], arrival[:, cut]) for cut in cuts], freq_count, write)


def make_spectrum(tile, rows, green, phasor, spectrum):
    freq_count = green.shape[2]
    lanes = 4 * BLOCK
    lane = lax.broadcasted_iota(jnp.int32, (2 * rows, 2 * lanes), 1) % BLOCK
    for block in range(freq_count // BLOCK):
        own = pl.ds(block * BLOCK, BLOCK)
        weights = jnp.concatenate([green[tile, c, own, :] for c in (0, 1, 2, 2, 3, 4, 5, 5)], axis=0)
        left = phasor[block * BLOCK * 2 * rows : (block + 1) * BLOCK * 2 * rows, :]
        product = lax.dot_general(
            left, weights, (((1,), (1,)), ((), ())), preferred_element_type=jnp.float32
        )
        picked = product[: 2 * rows]
        for k in range(1, BLOCK):
            picked = jnp.where(lane == k, product[k * 2 * rows : (k + 1) * 2 * rows], picked)
        real = picked[:rows, :lanes] - picked[rows:, lanes:]
        imag = picked[:rows, lanes:] + picked[rows:, :lanes]
        target = pl.ds(pl.multiple_of(tile * rows, rows), rows)
        spectrum[target, pl.ds(2 * block * lanes, lanes)] = real
        spectrum[target, pl.ds((2 * block + 1) * lanes, lanes)] = imag


def membership(ids, count, rupture, owner, row_count, rupture_total):
    tile_total = ids.shape[1]
    wide = row_count * rupture_total
    column = lax.broadcasted_iota(jnp.int32, (row_count, wide), 1)
    slot = lax.broadcasted_iota(jnp.int32, (row_count, 1), 0)
    pieces = []
    for tile in range(tile_total):
        place = owner[rupture[tile]] * row_count
        target = jnp.where(slot < count[tile], ids[:, tile : tile + 1] + place, -1)
        pieces.append((column == target).astype(jnp.float32))
    return jnp.concatenate(pieces, axis=0).astype(jnp.bfloat16)


def split(value):
    high = value.astype(jnp.bfloat16)
    return high, (value - high.astype(jnp.float32)).astype(jnp.bfloat16)


def route_rows(member, value):
    high, low = split(value)
    return lax.dot_general(
        jnp.concatenate([member, member], axis=0),
        jnp.concatenate([high, low], axis=0),
        (((0,), (0,)), ((), ())),
        preferred_element_type=jnp.float32,
    )


def inverse(total, table, freq_count):
    lanes = 4 * BLOCK
    rows = []
    for c in range(3):
        parts = []
        for part in range(2):
            for block in range(freq_count // BLOCK):
                at = (2 * block + part) * lanes + c * BLOCK
                parts.append(total[:, at : at + BLOCK])
        rows.append(jnp.concatenate(parts, axis=1))
    return jnp.dot(
        jnp.concatenate(rows, axis=0),
        table,
        precision=lax.Precision.HIGHEST,
        preferred_element_type=jnp.float32,
    )


def kernel(
    sites, devices, ids, count, rupture, owner, slip, time, table_hbm, green_hbm, out,
    green, table, maps, phasors, spectrum, member, partial, landed,
    green_sems, table_sem, map_send, map_recv, sum_send, sum_recv,
):
    tile_total, rows, local_points = slip.shape
    freq_count = green.shape[2]
    me = lax.axis_index("site")
    mine = lax.axis_index("fault")
    barrier = pltpu.get_barrier_semaphore()

    def greet_site(step, carry):
        peer = lax.rem(me + step, sites)
        pl.semaphore_signal(barrier, inc=1, device_id={"site": peer}, device_id_type=MESH)
        return carry

    def greet_fault(step, carry):
        peer = lax.rem(mine + step, devices)
        pl.semaphore_signal(barrier, inc=1, device_id={"fault": peer}, device_id_type=MESH)
        return carry

    lax.fori_loop(1, sites, greet_site, 0)
    lax.fori_loop(1, devices, greet_fault, 0)
    for tile in range(tile_total):
        pltpu.make_async_copy(green_hbm.at[tile], green.at[tile], green_sems.at[tile]).start()
    table_copy = pltpu.make_async_copy(table_hbm, table, table_sem)
    table_copy.start()
    maps[me] = jnp.concatenate([slip[...].astype(jnp.float32), time[...]], axis=2)
    pl.semaphore_wait(barrier, sites + devices - 2)

    chunk = tile_total // CHUNKS

    def map_copy(part, step):
        tiles = pl.ds(part * chunk, chunk)
        return pltpu.make_async_remote_copy(
            src_ref=maps.at[me, tiles],
            dst_ref=maps.at[me, tiles],
            send_sem=map_send.at[part, step],
            recv_sem=map_recv.at[part, me],
            device_id={"site": lax.rem(me + step, sites)},
            device_id_type=MESH,
        )

    def map_arrival(part, step):
        source = lax.rem(me + step, sites)
        tiles = pl.ds(part * chunk, chunk)
        return pltpu.make_async_remote_copy(
            src_ref=maps.at[source, tiles],
            dst_ref=maps.at[source, tiles],
            send_sem=map_send.at[part, step],
            recv_sem=map_recv.at[part, source],
            device_id={"site": source},
            device_id_type=MESH,
        )

    def over(first, last, body):
        lax.fori_loop(first, last, lambda step, carry: (body(step), carry)[1], 0)

    over(0, CHUNKS, lambda part: over(1, sites, lambda step: map_copy(part, step).start()))
    member[...] = membership(ids, count, rupture, owner, rows, owner.shape[0])

    def compute(part):
        over(1, sites, lambda step: map_arrival(part, step).wait_recv())

        def group(index):
            first = part * chunk + index * len(phasors)
            for at, phasor in enumerate(phasors):
                tile = first + at
                pltpu.make_async_copy(green_hbm.at[tile], green.at[tile], green_sems.at[tile]).wait()
            for at, phasor in enumerate(phasors):
                tile = first + at
                blocks = [maps[site, tile] for site in range(sites)]
                amplitude = jnp.concatenate([b[:, :local_points] for b in blocks], axis=1)
                arrival = jnp.concatenate([b[:, local_points:] for b in blocks], axis=1)
                make_phasors(amplitude, arrival, freq_count, phasor)
                make_spectrum(tile, rows, green, phasor, spectrum)

        over(0, chunk // len(phasors), group)

    over(0, CHUNKS, compute)
    routed = route_rows(member[...], spectrum[...])
    height = routed.shape[0] // devices
    for device in range(devices):
        partial[device] = routed[device * height : (device + 1) * height]

    def sum_copy(step):
        peer = lax.rem(mine + step, devices)
        return pltpu.make_async_remote_copy(
            src_ref=partial.at[peer],
            dst_ref=landed.at[mine],
            send_sem=sum_send.at[step],
            recv_sem=sum_recv.at[mine],
            device_id={"fault": peer},
            device_id_type=MESH,
        )

    def sum_arrival(step):
        source = lax.rem(mine + step, devices)
        return pltpu.make_async_remote_copy(
            src_ref=partial.at[source],
            dst_ref=landed.at[source],
            send_sem=sum_send.at[step],
            recv_sem=sum_recv.at[source],
            device_id={"fault": source},
            device_id_type=MESH,
        )

    over(1, devices, lambda step: sum_copy(step).start())
    table_copy.wait()
    total = partial[mine]
    for step in range(1, devices):
        sum_arrival(step).wait_recv()
        total = total + landed[lax.rem(mine + step, devices)]
    seismic = inverse(total, table[...], freq_count)
    for c in range(3):
        out[:, c, :] = seismic[c * height : (c + 1) * height]
    over(0, CHUNKS, lambda part: over(1, sites, lambda step: map_copy(part, step).wait_send()))
    over(1, devices, lambda step: sum_copy(step).wait_send())


def per_device(
    sites, devices,
    green_tensor, slip_map, rupture_time, variation_ids, variation_count, tile_rupture, owner_slot,
):
    green = jnp.swapaxes(green_tensor[0], 1, 2)
    tile_total, _, freq_count, points = green.shape
    rows, local_points = slip_map.shape[1:]
    rupture_total = owner_slot.shape[0]
    width = 8 * freq_count
    height = rupture_total * rows // devices
    smem = pl.BlockSpec(memory_space=pltpu.SMEM)
    vmem = pl.BlockSpec(memory_space=pltpu.VMEM)
    anywhere = pl.BlockSpec(memory_space=pl.ANY)
    dma = pltpu.SemaphoreType.DMA
    seismic = pl.pallas_call(
        functools.partial(kernel, sites, devices),
        out_shape=jax.ShapeDtypeStruct((height, 3, 2 * freq_count), jnp.float32),
        in_specs=[vmem, smem, smem, smem, vmem, vmem, anywhere, anywhere],
        out_specs=vmem,
        scratch_shapes=[
            pltpu.VMEM(green.shape, jnp.bfloat16),
            pltpu.VMEM((2 * freq_count, 2 * freq_count), jnp.float32),
            pltpu.VMEM((sites, tile_total, rows, 2 * local_points), jnp.float32),
            [pltpu.VMEM((freq_count * 2 * rows, points), jnp.bfloat16)] * UNROLL,
            pltpu.VMEM((tile_total * rows, width), jnp.float32),
            pltpu.VMEM((tile_total * rows, rupture_total * rows), jnp.bfloat16),
            pltpu.VMEM((devices, height, width), jnp.float32),
            pltpu.VMEM((devices, height, width), jnp.float32),
            dma((tile_total,)),
            dma(()),
            dma((CHUNKS, sites)),
            dma((CHUNKS, sites)),
            dma((devices,)),
            dma((devices,)),
        ],
        compiler_params=pltpu.CompilerParams(
            collective_id=0, has_side_effects=True, vmem_limit_bytes=60 * 1024 * 1024
        ),
        cost_estimate=pl.CostEstimate(flops=2 * 10**9, bytes_accessed=5 * 10**6, transcendentals=0),
    )(
        variation_ids.T, variation_count, tile_rupture, owner_slot,
        slip_map, rupture_time, inverse_table(freq_count), green,
    )
    return seismic.reshape(rupture_total // devices, rows, 1, 3, 2 * freq_count)


def solution(mesh):
    placed = (
        P("site", "fault", None, None, None),
        P("fault", None, "site"),
        P("fault", None, "site"),
        P("fault", None),
        P("fault"),
        P("fault"),
        P(),
    )
    return jax.shard_map(
        functools.partial(per_device, mesh.shape["site"], mesh.shape["fault"]),
        mesh=mesh,
        in_specs=placed,
        out_specs=P("fault", None, "site", None, None),
        check_vma=False,
    )
```

```python
import functools
import math

import jax
import jax.numpy as jnp
import numpy as np
from jax import lax
from jax.experimental import pallas as pl
from jax.experimental.pallas import tpu as pltpu
from jax.sharding import PartitionSpec as P

BLOCK = 32
HALF = 8
CHUNKS = 8
UNROLL = 2
MESH = pl.DeviceIdType.MESH


def inverse_table(freq_count):
    sample_count = 2 * freq_count
    wave = np.arange(freq_count)[:, None]
    sample = np.arange(sample_count)[None, :]
    angles = 2.0 * math.pi / sample_count * (wave * sample % sample_count)
    table = np.concatenate([np.cos(angles), -np.sin(angles)], axis=0) / math.sqrt(freq_count)
    return table.astype(np.float32)


def cos_sin(angle):
    x = angle - math.pi / 4
    y = x * x
    c = jnp.float32(1.0)
    s = jnp.float32(1.0)
    for n in (5, 4, 3, 2, 1):
        c = 1.0 - y * (c * (1.0 / ((2 * n - 1) * (2 * n))))
        s = 1.0 - y * (s * (1.0 / ((2 * n) * (2 * n + 1))))
    s = s * x
    root = math.sqrt(0.5)
    return root * (c - s), root * (c + s)


def turn(a, b):
    return a[0] * b[0] - a[1] * b[1], a[0] * b[1] + a[1] * b[0]


def phasor_blocks(pieces, freq_count, write):
    tables, steps, centres = [], [], []
    for amplitude, arrival in pieces:
        one = cos_sin(arrival * (2.0 * math.pi / (2 * freq_count)))
        one = (one[0], -one[1])
        powers = [None, one]
        for n in range(2, HALF + 1):
            powers.append(turn(powers[n // 2], powers[n - n // 2]))
        tables.append(powers)
        steps.append(turn(powers[HALF], powers[HALF]))
        centres.append((amplitude * powers[HALF][0], amplitude * powers[HALF][1]))
    for k in range(HALF, freq_count, 2 * HALF):
        for piece, powers in enumerate(tables):
            centre = centres[piece]
            write(k, piece, *centre)
            for n in range(1, HALF + 1):
                cc, ss = centre[0] * powers[n][0], centre[1] * powers[n][1]
                cs, sc = centre[0] * powers[n][1], centre[1] * powers[n][0]
                write(k - n, piece, cc + ss, sc - cs)
                if n < HALF:
                    write(k + n, piece, cc - ss, sc + cs)
            if k + 2 * HALF < freq_count:
                centres[piece] = turn(centre, steps[piece])


def make_phasors(amplitude, arrival, freq_count, phasor):
    rows, points = amplitude.shape
    lanes = 4 * BLOCK

    def write(k, piece, real, imag):
        both = jnp.concatenate([real, imag], axis=0).astype(jnp.bfloat16)
        phasor[k * 2 * rows : (k + 1) * 2 * rows, piece * lanes : (piece + 1) * lanes] = both

    cuts = [slice(at, at + lanes) for at in range(0, points, lanes)]
    phasor_blocks([(amplitude[:, cut], arrival[:, cut]) for cut in cuts], freq_count, write)


def split(value):
    high = value.astype(jnp.bfloat16)
    return high, (value - high.astype(jnp.float32)).astype(jnp.bfloat16)


def block_spectrum(tile, block, rows, green, phasor, spectrum):
    lanes = 4 * BLOCK
    lane = lax.broadcasted_iota(jnp.int32, (rows, lanes), 1) % BLOCK
    own = pl.ds(block * BLOCK, BLOCK)
    weights = jnp.concatenate([green[tile, c, own, :] for c in (0, 1, 2, 2, 3, 4, 5, 5)], axis=0)
    left = phasor[block * BLOCK * 2 * rows : (block + 1) * BLOCK * 2 * rows, :]
    product = lax.dot_general(
        left, weights, (((1,), (1,)), ((), ())), preferred_element_type=jnp.float32
    )
    picked = [None] * 4
    for k in range(BLOCK):
        here = lane == k
        for quarter in range(4):
            row, column = (2 * k + quarter // 2) * rows, quarter % 2 * lanes
            piece = product[row : row + rows, column : column + lanes]
            picked[quarter] = piece if k == 0 else jnp.where(here, piece, picked[quarter])
    real_high, real_low = split(picked[0] - picked[3])
    imag_high, imag_low = split(picked[1] + picked[2])
    target = pl.ds(pl.multiple_of(tile * 2 * rows, 2 * rows), 2 * rows)
    at = 2 * block * lanes
    spectrum[target, at : at + lanes] = jnp.concatenate([real_high, real_low], axis=0)
    spectrum[target, at + lanes : at + 2 * lanes] = jnp.concatenate([imag_high, imag_low], axis=0)


def membership(ids, count, rupture, owner, row_count, rupture_total):
    tile_total = ids.shape[1]
    wide = row_count * rupture_total
    column = lax.broadcasted_iota(jnp.int32, (row_count, wide), 1)
    slot = lax.broadcasted_iota(jnp.int32, (row_count, 1), 0)
    pieces = []
    for tile in range(tile_total):
        place = owner[rupture[tile]] * row_count
        target = jnp.where(slot < count[tile], ids[:, tile : tile + 1] + place, -1)
        pieces += [(column == target).astype(jnp.float32)] * 2
    return jnp.concatenate(pieces, axis=0).T.astype(jnp.bfloat16)


def route_rows(member, value):
    return jnp.dot(member, value, preferred_element_type=jnp.float32)


def inverse(total, table, freq_count):
    lanes = 4 * BLOCK
    rows = []
    for c in range(3):
        parts = []
        for part in range(2):
            for block in range(freq_count // BLOCK):
                at = (2 * block + part) * lanes + c * BLOCK
                parts.append(total[:, at : at + BLOCK])
        rows.append(jnp.concatenate(parts, axis=1))
    return jnp.dot(
        jnp.concatenate(rows, axis=0),
        table,
        precision=lax.Precision.HIGHEST,
        preferred_element_type=jnp.float32,
    )


def kernel(
    sites, devices,
    ids_hbm, count_hbm, rupture_hbm, owner_hbm, slip_hbm, time_hbm, table_hbm, green_hbm, out,
    ids, count, rupture, owner, slip, time, table, green,
    maps, phasors, spectrum, member, partial, landed,
    small_sems, green_sems, map_send, map_recv, sum_send, sum_recv,
):
    tile_total, rows, local_points = slip.shape
    freq_count = green.shape[2]
    me = lax.axis_index("site")
    mine = lax.axis_index("fault")
    barrier = pltpu.get_barrier_semaphore()

    def greet_site(step, carry):
        peer = lax.rem(me + step, sites)
        pl.semaphore_signal(barrier, inc=1, device_id={"site": peer}, device_id_type=MESH)
        return carry

    def greet_fault(step, carry):
        peer = lax.rem(mine + step, devices)
        pl.semaphore_signal(barrier, inc=1, device_id={"fault": peer}, device_id_type=MESH)
        return carry

    lax.fori_loop(1, sites, greet_site, 0)
    lax.fori_loop(1, devices, greet_fault, 0)
    pairs = (
        (slip_hbm, slip), (time_hbm, time), (ids_hbm, ids), (count_hbm, count),
        (rupture_hbm, rupture), (owner_hbm, owner), (table_hbm, table),
    )
    small = [pltpu.make_async_copy(a, b, small_sems.at[i]) for i, (a, b) in enumerate(pairs)]
    for copy in small[:-1]:
        copy.start()
    for tile in range(tile_total):
        pltpu.make_async_copy(green_hbm.at[tile], green.at[tile], green_sems.at[tile]).start()
    small[-1].start()
    for copy in small[:2]:
        copy.wait()
    maps[me] = jnp.concatenate([slip[...].astype(jnp.float32), time[...]], axis=2)
    pl.semaphore_wait(barrier, sites + devices - 2)

    chunk = tile_total // CHUNKS

    def map_copy(part, step):
        tiles = pl.ds(part * chunk, chunk)
        return pltpu.make_async_remote_copy(
            src_ref=maps.at[me, tiles],
            dst_ref=maps.at[me, tiles],
            send_sem=map_send.at[part, step],
            recv_sem=map_recv.at[part, me],
            device_id={"site": lax.rem(me + step, sites)},
            device_id_type=MESH,
        )

    def map_arrival(part, step):
        source = lax.rem(me + step, sites)
        tiles = pl.ds(part * chunk, chunk)
        return pltpu.make_async_remote_copy(
            src_ref=maps.at[source, tiles],
            dst_ref=maps.at[source, tiles],
            send_sem=map_send.at[part, step],
            recv_sem=map_recv.at[part, source],
            device_id={"site": source},
            device_id_type=MESH,
        )

    def over(first, last, body):
        lax.fori_loop(first, last, lambda step, carry: (body(step), carry)[1], 0)

    over(0, CHUNKS, lambda part: over(1, sites, lambda step: map_copy(part, step).start()))
    for copy in small[2:-1]:
        copy.wait()
    member[...] = membership(ids, count, rupture, owner, rows, owner.shape[0])

    def compute(part):
        over(1, sites, lambda step: map_arrival(part, step).wait_recv())

        def group(index):
            first = part * chunk + index * len(phasors)
            for at, phasor in enumerate(phasors):
                tile = first + at
                pltpu.make_async_copy(green_hbm.at[tile], green.at[tile], green_sems.at[tile]).wait()
            for at, phasor in enumerate(phasors):
                tile = first + at
                blocks = [maps[site, tile] for site in range(sites)]
                amplitude = jnp.concatenate([b[:, :local_points] for b in blocks], axis=1)
                arrival = jnp.concatenate([b[:, local_points:] for b in blocks], axis=1)
                make_phasors(amplitude, arrival, freq_count, phasor)
                for block in range(freq_count // BLOCK):
                    block_spectrum(tile, block, rows, green, phasor, spectrum)

        over(0, chunk // len(phasors), group)

    over(0, CHUNKS, compute)
    routed = route_rows(member[...], spectrum[...])
    height = routed.shape[0] // devices
    for device in range(devices):
        partial[device] = routed[device * height : (device + 1) * height]

    def sum_copy(step):
        peer = lax.rem(mine + step, devices)
        return pltpu.make_async_remote_copy(
            src_ref=partial.at[peer],
            dst_ref=landed.at[mine],
            send_sem=sum_send.at[step],
            recv_sem=sum_recv.at[mine],
            device_id={"fault": peer},
            device_id_type=MESH,
        )

    def sum_arrival(step):
        source = lax.rem(mine + step, devices)
        return pltpu.make_async_remote_copy(
            src_ref=partial.at[source],
            dst_ref=landed.at[source],
            send_sem=sum_send.at[step],
            recv_sem=sum_recv.at[source],
            device_id={"fault": source},
            device_id_type=MESH,
        )

    over(1, devices, lambda step: sum_copy(step).start())
    small[-1].wait()
    total = partial[mine]
    for step in range(1, devices):
        sum_arrival(step).wait_recv()
        total = total + landed[lax.rem(mine + step, devices)]
    seismic = inverse(total, table[...], freq_count)
    for c in range(3):
        for row in range(height):
            at = c * height + row
            out[row, c] = seismic[at : at + 1]
    over(0, CHUNKS, lambda part: over(1, sites, lambda step: map_copy(part, step).wait_send()))
    over(1, devices, lambda step: sum_copy(step).wait_send())


def per_device(
    sites, devices,
    green_tensor, slip_map, rupture_time, variation_ids, variation_count, tile_rupture, owner_slot,
):
    green = jnp.swapaxes(green_tensor[0], 1, 2)
    tile_total, _, freq_count, points = green.shape
    rows, local_points = slip_map.shape[1:]
    rupture_total = owner_slot.shape[0]
    width = 8 * freq_count
    height = rupture_total * rows // devices
    vmem = pl.BlockSpec(memory_space=pltpu.VMEM)
    anywhere = pl.BlockSpec(memory_space=pl.ANY)
    dma = pltpu.SemaphoreType.DMA
    seismic = pl.pallas_call(
        functools.partial(kernel, sites, devices),
        out_shape=jax.ShapeDtypeStruct((height, 3, 1, 2 * freq_count), jnp.float32),
        in_specs=[anywhere] * 8,
        out_specs=vmem,
        scratch_shapes=[
            pltpu.VMEM((rows, tile_total), jnp.int32),
            pltpu.SMEM((tile_total,), jnp.int32),
            pltpu.SMEM((tile_total,), jnp.int32),
            pltpu.SMEM((rupture_total,), jnp.int32),
            pltpu.VMEM(slip_map.shape, slip_map.dtype),
            pltpu.VMEM(rupture_time.shape, jnp.float32),
            pltpu.VMEM((2 * freq_count, 2 * freq_count), jnp.float32),
            pltpu.VMEM(green.shape, jnp.bfloat16),
            pltpu.VMEM((sites, tile_total, rows, 2 * local_points), jnp.float32),
            [pltpu.VMEM((freq_count * 2 * rows, points), jnp.bfloat16)] * UNROLL,
            pltpu.VMEM((tile_total * 2 * rows, width), jnp.bfloat16),
            pltpu.VMEM((rupture_total * rows, tile_total * 2 * rows), jnp.bfloat16),
            pltpu.VMEM((devices, height, width), jnp.float32),
            pltpu.VMEM((devices, height, width), jnp.float32),
            dma((7,)),
            dma((tile_total,)),
            dma((CHUNKS, sites)),
            dma((CHUNKS, sites)),
            dma((devices,)),
            dma((devices,)),
        ],
        compiler_params=pltpu.CompilerParams(
            collective_id=0, has_side_effects=True, vmem_limit_bytes=60 * 1024 * 1024
        ),
        cost_estimate=pl.CostEstimate(flops=2 * 10**9, bytes_accessed=5 * 10**6, transcendentals=0),
    )(
        variation_ids.T, variation_count, tile_rupture, owner_slot,
        slip_map, rupture_time, inverse_table(freq_count), green,
    )
    seismic = seismic.reshape(rupture_total // devices, rows, 3, 1, 2 * freq_count)
    return jnp.swapaxes(seismic, 2, 3)


def solution(mesh):
    placed = (
        P("site", "fault", None, None, None),
        P("fault", None, "site"),
        P("fault", None, "site"),
        P("fault", None),
        P("fault"),
        P("fault"),
        P(),
    )
    return jax.shard_map(
        functools.partial(per_device, mesh.shape["site"], mesh.shape["fault"]),
        mesh=mesh,
        in_specs=placed,
        out_specs=P("fault", None, "site", None, None),
        check_vma=False,
    )
```

```python
import functools
import math

import jax
import jax.numpy as jnp
import numpy as np
from jax import lax
from jax.experimental import pallas as pl
from jax.experimental.pallas import tpu as pltpu
from jax.sharding import PartitionSpec as P

BLOCK = 32
HALF = 8
CHUNK = 2
MESH = pl.DeviceIdType.MESH


def inverse_table(freq_count):
    sample_count = 2 * freq_count
    wave = np.arange(freq_count)[:, None]
    sample = np.arange(sample_count)[None, :]
    angles = 2.0 * math.pi / sample_count * (wave * sample % sample_count)
    table = np.concatenate([np.cos(angles), -np.sin(angles)], axis=0) / math.sqrt(freq_count)
    return table.astype(np.float32)


def cos_sin(angle):
    x = angle - math.pi / 4
    y = x * x
    c = jnp.float32(1.0)
    s = jnp.float32(1.0)
    for n in (5, 4, 3, 2, 1):
        c = 1.0 - y * (c * (1.0 / ((2 * n - 1) * (2 * n))))
        s = 1.0 - y * (s * (1.0 / ((2 * n) * (2 * n + 1))))
    s = s * x
    root = math.sqrt(0.5)
    return root * (c - s), root * (c + s)


def turn(a, b):
    return a[0] * b[0] - a[1] * b[1], a[0] * b[1] + a[1] * b[0]


def phasor_blocks(pieces, freq_count, write):
    tables, steps, centres = [], [], []
    for amplitude, arrival in pieces:
        one = cos_sin(arrival * (2.0 * math.pi / (2 * freq_count)))
        one = (one[0], -one[1])
        powers = [None, one]
        for n in range(2, HALF + 1):
            powers.append(turn(powers[n // 2], powers[n - n // 2]))
        tables.append(powers)
        steps.append(turn(powers[HALF], powers[HALF]))
        centres.append((amplitude * powers[HALF][0], amplitude * powers[HALF][1]))
    for k in range(HALF, freq_count, 2 * HALF):
        for piece, powers in enumerate(tables):
            centre = centres[piece]
            write(k, piece, *centre)
            for n in range(1, HALF + 1):
                cc, ss = centre[0] * powers[n][0], centre[1] * powers[n][1]
                cs, sc = centre[0] * powers[n][1], centre[1] * powers[n][0]
                write(k - n, piece, cc + ss, sc - cs)
                if n < HALF:
                    write(k + n, piece, cc - ss, sc + cs)
            if k + 2 * HALF < freq_count:
                centres[piece] = turn(centre, steps[piece])
        yield


def make_phasors(amplitude, arrival, freq_count, phasor):
    rows, points = amplitude.shape
    lanes = 4 * BLOCK

    def write(k, piece, real, imag):
        both = jnp.concatenate([real, imag], axis=0).astype(jnp.bfloat16)
        phasor[k * 2 * rows : (k + 1) * 2 * rows, piece * lanes : (piece + 1) * lanes] = both

    cuts = [slice(at, at + lanes) for at in range(0, points, lanes)]
    return phasor_blocks([(amplitude[:, cut], arrival[:, cut]) for cut in cuts], freq_count, write)


def split(value):
    high = value.astype(jnp.bfloat16)
    return high, (value - high.astype(jnp.float32)).astype(jnp.bfloat16)


def block_spectrum(tile, block, rows, green, phasor, spectrum):
    lanes = 4 * BLOCK
    lane = lax.broadcasted_iota(jnp.int32, (rows, lanes), 1) % BLOCK
    own = pl.ds(block * BLOCK, BLOCK)
    weights = jnp.concatenate([green[tile, c, own, :] for c in (0, 1, 2, 2, 3, 4, 5, 5)], axis=0)
    left = phasor[block * BLOCK * 2 * rows : (block + 1) * BLOCK * 2 * rows, :]
    product = lax.dot_general(
        left, weights, (((1,), (1,)), ((), ())), preferred_element_type=jnp.float32
    )
    picked = [None] * 4
    for k in range(BLOCK):
        here = lane == k
        for quarter in range(4):
            row, column = (2 * k + quarter // 2) * rows, quarter % 2 * lanes
            piece = product[row : row + rows, column : column + lanes]
            picked[quarter] = piece if k == 0 else jnp.where(here, piece, picked[quarter])
    real_high, real_low = split(picked[0] - picked[3])
    imag_high, imag_low = split(picked[1] + picked[2])
    target = pl.ds(pl.multiple_of(tile * 2 * rows, 2 * rows), 2 * rows)
    at = 2 * block * lanes
    spectrum[target, at : at + lanes] = jnp.concatenate([real_high, real_low], axis=0)
    spectrum[target, at + lanes : at + 2 * lanes] = jnp.concatenate([imag_high, imag_low], axis=0)


def membership(ids, count, rupture, owner, row_count, rupture_total):
    tile_total = ids.shape[1]
    wide = row_count * rupture_total
    column = lax.broadcasted_iota(jnp.int32, (row_count, wide), 1)
    slot = lax.broadcasted_iota(jnp.int32, (row_count, 1), 0)
    pieces = []
    for tile in range(tile_total):
        place = owner[rupture[tile]] * row_count
        target = jnp.where(slot < count[tile], ids[:, tile : tile + 1] + place, -1)
        pieces += [(column == target).astype(jnp.float32)] * 2
    return jnp.concatenate(pieces, axis=0).T.astype(jnp.bfloat16)


def route_rows(member, value):
    return jnp.dot(member, value, preferred_element_type=jnp.float32)


def inverse(total, table, freq_count):
    lanes = 4 * BLOCK
    rows = []
    for c in range(3):
        parts = []
        for part in range(2):
            for block in range(freq_count // BLOCK):
                at = (2 * block + part) * lanes + c * BLOCK
                parts.append(total[:, at : at + BLOCK])
        rows.append(jnp.concatenate(parts, axis=1))
    return jnp.dot(
        jnp.concatenate(rows, axis=0),
        table,
        precision=lax.Precision.HIGHEST,
        preferred_element_type=jnp.float32,
    )


def kernel(
    sites, devices,
    ids_hbm, count_hbm, rupture_hbm, owner_hbm, slip_hbm, time_hbm, table_hbm, green_hbm, out,
    ids, count, rupture, owner, slip, time, table, green,
    maps, phasors, spectrum, member, partial, landed,
    small_sems, green_sems, map_send, map_recv, sum_send, sum_recv,
):
    tile_total, rows, local_points = slip.shape
    freq_count = green.shape[2]
    me = lax.axis_index("site")
    mine = lax.axis_index("fault")
    barrier = pltpu.get_barrier_semaphore()

    def greet_site(step, carry):
        peer = lax.rem(me + step, sites)
        pl.semaphore_signal(barrier, inc=1, device_id={"site": peer}, device_id_type=MESH)
        return carry

    def greet_fault(step, carry):
        peer = lax.rem(mine + step, devices)
        pl.semaphore_signal(barrier, inc=1, device_id={"fault": peer}, device_id_type=MESH)
        return carry

    lax.fori_loop(1, sites, greet_site, 0)
    lax.fori_loop(1, devices, greet_fault, 0)
    pairs = (
        (slip_hbm, slip), (time_hbm, time), (ids_hbm, ids), (count_hbm, count),
        (rupture_hbm, rupture), (owner_hbm, owner), (table_hbm, table),
    )
    small = [pltpu.make_async_copy(a, b, small_sems.at[i]) for i, (a, b) in enumerate(pairs)]
    for copy in small[:-1]:
        copy.start()
    for tile in range(tile_total):
        pltpu.make_async_copy(green_hbm.at[tile], green.at[tile], green_sems.at[tile]).start()
    small[-1].start()
    for copy in small[:2]:
        copy.wait()
    maps[me] = jnp.concatenate([slip[...].astype(jnp.float32), time[...]], axis=2)
    pl.semaphore_wait(barrier, sites + devices - 2)

    chunk = CHUNK
    chunks = tile_total // CHUNK

    def map_copy(part, step):
        tiles = pl.ds(part * chunk, chunk)
        return pltpu.make_async_remote_copy(
            src_ref=maps.at[me, tiles],
            dst_ref=maps.at[me, tiles],
            send_sem=map_send.at[part, step],
            recv_sem=map_recv.at[part, me],
            device_id={"site": lax.rem(me + step, sites)},
            device_id_type=MESH,
        )

    def map_arrival(part, step):
        source = lax.rem(me + step, sites)
        tiles = pl.ds(part * chunk, chunk)
        return pltpu.make_async_remote_copy(
            src_ref=maps.at[source, tiles],
            dst_ref=maps.at[source, tiles],
            send_sem=map_send.at[part, step],
            recv_sem=map_recv.at[part, source],
            device_id={"site": source},
            device_id_type=MESH,
        )

    def over(first, last, body):
        lax.fori_loop(first, last, lambda step, carry: (body(step), carry)[1], 0)

    over(0, chunks, lambda part: over(1, sites, lambda step: map_copy(part, step).start()))
    for copy in small[2:-1]:
        copy.wait()
    member[...] = membership(ids, count, rupture, owner, rows, owner.shape[0])

    def arrive(part):
        over(1, sites, lambda step: map_arrival(part, step).wait_recv())

    def phasor_steps(tile, phasor):
        blocks = [maps[site, tile] for site in range(sites)]
        amplitude = jnp.concatenate([b[:, :local_points] for b in blocks], axis=1)
        arrival = jnp.concatenate([b[:, local_points:] for b in blocks], axis=1)
        return make_phasors(amplitude, arrival, freq_count, phasor)

    def dot_steps(tile, phasor):
        pltpu.make_async_copy(green_hbm.at[tile], green.at[tile], green_sems.at[tile]).wait()
        for block in range(freq_count // BLOCK):
            yield
            block_spectrum(tile, block, rows, green, phasor, spectrum)

    def alternate(*works):
        works = list(works)
        while works:
            works = [work for work in works if next(work, works) is not works]

    def pair(index):
        first = index * chunk
        alternate(dot_steps(first, phasors[0]), phasor_steps(first + 1, phasors[1]))
        arrive(index + 1)
        alternate(dot_steps(first + 1, phasors[1]), phasor_steps(first + 2, phasors[0]))

    arrive(0)
    alternate(phasor_steps(0, phasors[0]))
    over(0, chunks - 1, pair)
    last = tile_total - 2
    alternate(dot_steps(last, phasors[0]), phasor_steps(last + 1, phasors[1]))
    alternate(dot_steps(last + 1, phasors[1]))
    routed = route_rows(member[...], spectrum[...])
    height = routed.shape[0] // devices
    for device in range(devices):
        partial[device] = routed[device * height : (device + 1) * height]

    def sum_copy(step):
        peer = lax.rem(mine + step, devices)
        return pltpu.make_async_remote_copy(
            src_ref=partial.at[peer],
            dst_ref=landed.at[mine],
            send_sem=sum_send.at[step],
            recv_sem=sum_recv.at[mine],
            device_id={"fault": peer},
            device_id_type=MESH,
        )

    def sum_arrival(step):
        source = lax.rem(mine + step, devices)
        return pltpu.make_async_remote_copy(
            src_ref=partial.at[source],
            dst_ref=landed.at[source],
            send_sem=sum_send.at[step],
            recv_sem=sum_recv.at[source],
            device_id={"fault": source},
            device_id_type=MESH,
        )

    over(1, devices, lambda step: sum_copy(step).start())
    small[-1].wait()
    total = partial[mine]
    for step in range(1, devices):
        sum_arrival(step).wait_recv()
        total = total + landed[lax.rem(mine + step, devices)]
    seismic = inverse(total, table[...], freq_count)
    for c in range(3):
        for row in range(height):
            at = c * height + row
            out[row, c] = seismic[at : at + 1]
    over(0, chunks, lambda part: over(1, sites, lambda step: map_copy(part, step).wait_send()))
    over(1, devices, lambda step: sum_copy(step).wait_send())


def per_device(
    sites, devices,
    green_tensor, slip_map, rupture_time, variation_ids, variation_count, tile_rupture, owner_slot,
):
    green = jnp.swapaxes(green_tensor[0], 1, 2)
    tile_total, _, freq_count, points = green.shape
    rows, local_points = slip_map.shape[1:]
    rupture_total = owner_slot.shape[0]
    width = 8 * freq_count
    height = rupture_total * rows // devices
    vmem = pl.BlockSpec(memory_space=pltpu.VMEM)
    anywhere = pl.BlockSpec(memory_space=pl.ANY)
    dma = pltpu.SemaphoreType.DMA
    seismic = pl.pallas_call(
        functools.partial(kernel, sites, devices),
        out_shape=jax.ShapeDtypeStruct((height, 3, 1, 2 * freq_count), jnp.float32),
        in_specs=[anywhere] * 8,
        out_specs=vmem,
        scratch_shapes=[
            pltpu.VMEM((rows, tile_total), jnp.int32),
            pltpu.SMEM((tile_total,), jnp.int32),
            pltpu.SMEM((tile_total,), jnp.int32),
            pltpu.SMEM((rupture_total,), jnp.int32),
            pltpu.VMEM(slip_map.shape, slip_map.dtype),
            pltpu.VMEM(rupture_time.shape, jnp.float32),
            pltpu.VMEM((2 * freq_count, 2 * freq_count), jnp.float32),
            pltpu.VMEM(green.shape, jnp.bfloat16),
            pltpu.VMEM((sites, tile_total, rows, 2 * local_points), jnp.float32),
            [pltpu.VMEM((freq_count * 2 * rows, points), jnp.bfloat16)] * 2,
            pltpu.VMEM((tile_total * 2 * rows, width), jnp.bfloat16),
            pltpu.VMEM((rupture_total * rows, tile_total * 2 * rows), jnp.bfloat16),
            pltpu.VMEM((devices, height, width), jnp.float32),
            pltpu.VMEM((devices, height, width), jnp.float32),
            dma((7,)),
            dma((tile_total,)),
            dma((tile_total // CHUNK, sites)),
            dma((tile_total // CHUNK, sites)),
            dma((devices,)),
            dma((devices,)),
        ],
        compiler_params=pltpu.CompilerParams(
            collective_id=0, has_side_effects=True, vmem_limit_bytes=60 * 1024 * 1024
        ),
        cost_estimate=pl.CostEstimate(flops=2 * 10**9, bytes_accessed=5 * 10**6, transcendentals=0),
    )(
        variation_ids.T, variation_count, tile_rupture, owner_slot,
        slip_map, rupture_time, inverse_table(freq_count), green,
    )
    seismic = seismic.reshape(rupture_total // devices, rows, 3, 1, 2 * freq_count)
    return jnp.swapaxes(seismic, 2, 3)


def solution(mesh):
    placed = (
        P("site", "fault", None, None, None),
        P("fault", None, "site"),
        P("fault", None, "site"),
        P("fault", None),
        P("fault"),
        P("fault"),
        P(),
    )
    return jax.shard_map(
        functools.partial(per_device, mesh.shape["site"], mesh.shape["fault"]),
        mesh=mesh,
        in_specs=placed,
        out_specs=P("fault", None, "site", None, None),
        check_vma=False,
    )
```

```python
import functools
import math

import jax
import jax.numpy as jnp
import numpy as np
from jax import lax
from jax.experimental import pallas as pl
from jax.experimental.pallas import tpu as pltpu
from jax.sharding import PartitionSpec as P

BLOCK = 32
HALF = 8
CHUNKS = 8
UNROLL = 2
MESH = pl.DeviceIdType.MESH


def inverse_table(freq_count):
    sample_count = 2 * freq_count
    wave = np.arange(freq_count)[:, None]
    sample = np.arange(sample_count)[None, :]
    angles = 2.0 * math.pi / sample_count * (wave * sample % sample_count)
    table = np.concatenate([np.cos(angles), -np.sin(angles)], axis=0) / math.sqrt(freq_count)
    return table.astype(np.float32)


def cos_sin(angle):
    x = angle - math.pi / 4
    y = x * x
    c = jnp.float32(1.0)
    s = jnp.float32(1.0)
    for n in (5, 4, 3, 2, 1):
        c = 1.0 - y * (c * (1.0 / ((2 * n - 1) * (2 * n))))
        s = 1.0 - y * (s * (1.0 / ((2 * n) * (2 * n + 1))))
    s = s * x
    root = math.sqrt(0.5)
    return root * (c - s), root * (c + s)


def turn(a, b):
    return a[0] * b[0] - a[1] * b[1], a[0] * b[1] + a[1] * b[0]


def phasor_blocks(amplitude, arrival, freq_count, write):
    one = cos_sin(arrival * (2.0 * math.pi / (2 * freq_count)))
    one = (one[0], -one[1])
    powers = [None, one]
    for n in range(2, HALF + 1):
        powers.append(turn(powers[n // 2], powers[n - n // 2]))
    step = turn(powers[HALF], powers[HALF])
    centre = (amplitude * powers[HALF][0], amplitude * powers[HALF][1])
    for k in range(HALF, freq_count, 2 * HALF):
        for n in range(1, HALF + 1):
            cc, ss = centre[0] * powers[n][0], centre[1] * powers[n][1]
            cs, sc = centre[0] * powers[n][1], centre[1] * powers[n][0]
            upper = (cc - ss, sc + cs) if n < HALF else centre
            write(k, n, ((cc + ss, sc - cs), upper))
        if k + 2 * HALF < freq_count:
            centre = turn(centre, step)


def frequency_order(block):
    order = []
    for k in range(block * BLOCK + HALF, (block + 1) * BLOCK, 2 * HALF):
        for n in range(1, HALF + 1):
            order += [k - n, k + n if n < HALF else k]
    return order


def make_phasors(amplitude, arrival, freq_count, phasor):
    rows, points = amplitude.shape
    lanes = 4 * BLOCK
    for start in range(0, points, lanes):

        def write(k, n, values):
            row = (k - HALF + 2 * (n - 1)) * rows
            for part in range(2):
                both = jnp.concatenate([values[0][part], values[1][part]], axis=0)
                at = part * points + start
                phasor[row : row + 2 * rows, at : at + lanes] = both.astype(jnp.bfloat16)

        cut = slice(start, start + lanes)
        phasor_blocks(amplitude[:, cut], arrival[:, cut], freq_count, write)


def split(value):
    high = value.astype(jnp.bfloat16)
    return high, (value - high.astype(jnp.float32)).astype(jnp.bfloat16)


def block_spectrum(tile, block, rows, green, phasor, spectrum):
    lanes = 4 * BLOCK
    lane = lax.broadcasted_iota(jnp.int32, (rows, lanes), 1) % BLOCK
    own = pl.ds(block * BLOCK, BLOCK)
    real = [green[tile, c, own, :] for c in (0, 1, 2, 2)]
    imag = [green[tile, c, own, :] for c in (3, 4, 5, 5)]
    weights = jnp.concatenate(
        [
            jnp.concatenate(real + imag, axis=0),
            jnp.concatenate([-g for g in imag] + real, axis=0),
        ],
        axis=1,
    )
    left = phasor[block * BLOCK * rows : (block + 1) * BLOCK * rows, :]
    product = lax.dot_general(
        left, weights, (((1,), (1,)), ((), ())), preferred_element_type=jnp.float32
    )
    picked = [None] * 2
    for place, k in enumerate(frequency_order(block)):
        here = lane == k % BLOCK
        for part in range(2):
            piece = product[place * rows : (place + 1) * rows, part * lanes : (part + 1) * lanes]
            picked[part] = piece if place == 0 else jnp.where(here, piece, picked[part])
    real_high, real_low = split(picked[0])
    imag_high, imag_low = split(picked[1])
    target = pl.ds(pl.multiple_of(tile * 2 * rows, 2 * rows), 2 * rows)
    at = 2 * block * lanes
    spectrum[target, at : at + lanes] = jnp.concatenate([real_high, real_low], axis=0)
    spectrum[target, at + lanes : at + 2 * lanes] = jnp.concatenate([imag_high, imag_low], axis=0)


def membership(ids, count, rupture, owner, row_count, rupture_total):
    tile_total = ids.shape[1]
    wide = row_count * rupture_total
    column = lax.broadcasted_iota(jnp.int32, (row_count, wide), 1)
    slot = lax.broadcasted_iota(jnp.int32, (row_count, 1), 0)
    pieces = []
    for tile in range(tile_total):
        place = owner[rupture[tile]] * row_count
        target = jnp.where(slot < count[tile], ids[:, tile : tile + 1] + place, -1)
        pieces += [(column == target).astype(jnp.float32)] * 2
    return jnp.concatenate(pieces, axis=0).T.astype(jnp.bfloat16)


def route_rows(member, value):
    return jnp.dot(member, value, preferred_element_type=jnp.float32)


def inverse(total, table, freq_count):
    lanes = 4 * BLOCK
    rows = []
    for c in range(3):
        parts = []
        for part in range(2):
            for block in range(freq_count // BLOCK):
                at = (2 * block + part) * lanes + c * BLOCK
                parts.append(total[:, at : at + BLOCK])
        rows.append(jnp.concatenate(parts, axis=1))
    return jnp.dot(
        jnp.concatenate(rows, axis=0),
        table,
        precision=lax.Precision.HIGHEST,
        preferred_element_type=jnp.float32,
    )


def kernel(
    sites, devices,
    ids_hbm, count_hbm, rupture_hbm, owner_hbm, slip_hbm, time_hbm, table_hbm, green_hbm, out,
    ids, count, rupture, owner, slip, time, table, green,
    maps, phasors, spectrum, member, partial, landed,
    small_sems, green_sems, map_send, map_recv, sum_send, sum_recv,
):
    tile_total, rows, local_points = slip.shape
    freq_count = green.shape[2]
    me = lax.axis_index("site")
    mine = lax.axis_index("fault")
    barrier = pltpu.get_barrier_semaphore()

    def greet_site(step, carry):
        peer = lax.rem(me + step, sites)
        pl.semaphore_signal(barrier, inc=1, device_id={"site": peer}, device_id_type=MESH)
        return carry

    def greet_fault(step, carry):
        peer = lax.rem(mine + step, devices)
        pl.semaphore_signal(barrier, inc=1, device_id={"fault": peer}, device_id_type=MESH)
        return carry

    lax.fori_loop(1, sites, greet_site, 0)
    lax.fori_loop(1, devices, greet_fault, 0)
    pairs = (
        (slip_hbm, slip), (time_hbm, time), (ids_hbm, ids), (count_hbm, count),
        (rupture_hbm, rupture), (owner_hbm, owner), (table_hbm, table),
    )
    small = [pltpu.make_async_copy(a, b, small_sems.at[i]) for i, (a, b) in enumerate(pairs)]
    for copy in small[:-1]:
        copy.start()
    for tile in range(tile_total):
        pltpu.make_async_copy(green_hbm.at[tile], green.at[tile], green_sems.at[tile]).start()
    small[-1].start()
    for copy in small[:2]:
        copy.wait()
    maps[me] = jnp.concatenate([slip[...].astype(jnp.float32), time[...]], axis=2)
    pl.semaphore_wait(barrier, sites + devices - 2)

    chunk = tile_total // CHUNKS

    def map_copy(part, step):
        tiles = pl.ds(part * chunk, chunk)
        return pltpu.make_async_remote_copy(
            src_ref=maps.at[me, tiles],
            dst_ref=maps.at[me, tiles],
            send_sem=map_send.at[part, step],
            recv_sem=map_recv.at[part, me],
            device_id={"site": lax.rem(me + step, sites)},
            device_id_type=MESH,
        )

    def map_arrival(part, step):
        source = lax.rem(me + step, sites)
        tiles = pl.ds(part * chunk, chunk)
        return pltpu.make_async_remote_copy(
            src_ref=maps.at[source, tiles],
            dst_ref=maps.at[source, tiles],
            send_sem=map_send.at[part, step],
            recv_sem=map_recv.at[part, source],
            device_id={"site": source},
            device_id_type=MESH,
        )

    def over(first, last, body):
        lax.fori_loop(first, last, lambda step, carry: (body(step), carry)[1], 0)

    over(0, CHUNKS, lambda part: over(1, sites, lambda step: map_copy(part, step).start()))
    for copy in small[2:-1]:
        copy.wait()
    member[...] = membership(ids, count, rupture, owner, rows, owner.shape[0])

    def compute(part):
        over(1, sites, lambda step: map_arrival(part, step).wait_recv())

        def group(index):
            first = part * chunk + index * len(phasors)
            for at, phasor in enumerate(phasors):
                tile = first + at
                pltpu.make_async_copy(green_hbm.at[tile], green.at[tile], green_sems.at[tile]).wait()
            for at, phasor in enumerate(phasors):
                tile = first + at
                blocks = [maps[site, tile] for site in range(sites)]
                amplitude = jnp.concatenate([b[:, :local_points] for b in blocks], axis=1)
                arrival = jnp.concatenate([b[:, local_points:] for b in blocks], axis=1)
                make_phasors(amplitude, arrival, freq_count, phasor)
                for block in range(freq_count // BLOCK):
                    block_spectrum(tile, block, rows, green, phasor, spectrum)

        over(0, chunk // len(phasors), group)

    over(0, CHUNKS, compute)
    routed = route_rows(member[...], spectrum[...])
    height = routed.shape[0] // devices
    for device in range(devices):
        partial[device] = routed[device * height : (device + 1) * height]

    def sum_copy(step):
        peer = lax.rem(mine + step, devices)
        return pltpu.make_async_remote_copy(
            src_ref=partial.at[peer],
            dst_ref=landed.at[mine],
            send_sem=sum_send.at[step],
            recv_sem=sum_recv.at[mine],
            device_id={"fault": peer},
            device_id_type=MESH,
        )

    def sum_arrival(step):
        source = lax.rem(mine + step, devices)
        return pltpu.make_async_remote_copy(
            src_ref=partial.at[source],
            dst_ref=landed.at[source],
            send_sem=sum_send.at[step],
            recv_sem=sum_recv.at[source],
            device_id={"fault": source},
            device_id_type=MESH,
        )

    over(1, devices, lambda step: sum_copy(step).start())
    small[-1].wait()
    total = partial[mine]
    for step in range(1, devices):
        sum_arrival(step).wait_recv()
        total = total + landed[lax.rem(mine + step, devices)]
    seismic = inverse(total, table[...], freq_count)
    for c in range(3):
        for row in range(height):
            at = c * height + row
            out[row, c] = seismic[at : at + 1]
    over(0, CHUNKS, lambda part: over(1, sites, lambda step: map_copy(part, step).wait_send()))
    over(1, devices, lambda step: sum_copy(step).wait_send())


def per_device(
    sites, devices,
    green_tensor, slip_map, rupture_time, variation_ids, variation_count, tile_rupture, owner_slot,
):
    green = jnp.swapaxes(green_tensor[0], 1, 2)
    tile_total, _, freq_count, points = green.shape
    rows, local_points = slip_map.shape[1:]
    rupture_total = owner_slot.shape[0]
    width = 8 * freq_count
    height = rupture_total * rows // devices
    vmem = pl.BlockSpec(memory_space=pltpu.VMEM)
    anywhere = pl.BlockSpec(memory_space=pl.ANY)
    dma = pltpu.SemaphoreType.DMA
    seismic = pl.pallas_call(
        functools.partial(kernel, sites, devices),
        out_shape=jax.ShapeDtypeStruct((height, 3, 1, 2 * freq_count), jnp.float32),
        in_specs=[anywhere] * 8,
        out_specs=vmem,
        scratch_shapes=[
            pltpu.VMEM((rows, tile_total), jnp.int32),
            pltpu.SMEM((tile_total,), jnp.int32),
            pltpu.SMEM((tile_total,), jnp.int32),
            pltpu.SMEM((rupture_total,), jnp.int32),
            pltpu.VMEM(slip_map.shape, slip_map.dtype),
            pltpu.VMEM(rupture_time.shape, jnp.float32),
            pltpu.VMEM((2 * freq_count, 2 * freq_count), jnp.float32),
            pltpu.VMEM(green.shape, jnp.bfloat16),
            pltpu.VMEM((sites, tile_total, rows, 2 * local_points), jnp.float32),
            [pltpu.VMEM((freq_count * rows, 2 * points), jnp.bfloat16)] * UNROLL,
            pltpu.VMEM((tile_total * 2 * rows, width), jnp.bfloat16),
            pltpu.VMEM((rupture_total * rows, tile_total * 2 * rows), jnp.bfloat16),
            pltpu.VMEM((devices, height, width), jnp.float32),
            pltpu.VMEM((devices, height, width), jnp.float32),
            dma((7,)),
            dma((tile_total,)),
            dma((CHUNKS, sites)),
            dma((CHUNKS, sites)),
            dma((devices,)),
            dma((devices,)),
        ],
        compiler_params=pltpu.CompilerParams(
            collective_id=0, has_side_effects=True, vmem_limit_bytes=60 * 1024 * 1024
        ),
        cost_estimate=pl.CostEstimate(flops=2 * 10**9, bytes_accessed=5 * 10**6, transcendentals=0),
    )(
        variation_ids.T, variation_count, tile_rupture, owner_slot,
        slip_map, rupture_time, inverse_table(freq_count), green,
    )
    seismic = seismic.reshape(rupture_total // devices, rows, 3, 1, 2 * freq_count)
    return jnp.swapaxes(seismic, 2, 3)


def solution(mesh):
    placed = (
        P("site", "fault", None, None, None),
        P("fault", None, "site"),
        P("fault", None, "site"),
        P("fault", None),
        P("fault"),
        P("fault"),
        P(),
    )
    return jax.shard_map(
        functools.partial(per_device, mesh.shape["site"], mesh.shape["fault"]),
        mesh=mesh,
        in_specs=placed,
        out_specs=P("fault", None, "site", None, None),
        check_vma=False,
    )
```

```python
import functools
import math

import jax
import jax.numpy as jnp
import numpy as np
from jax import lax
from jax.experimental import pallas as pl
from jax.experimental.pallas import tpu as pltpu
from jax.sharding import PartitionSpec as P

BLOCK = 32
HALF = 8
CHUNKS = 8
AHEAD = 2
UNROLL = 2
MESH = pl.DeviceIdType.MESH


def inverse_table(freq_count):
    sample_count = 2 * freq_count
    wave = np.arange(freq_count)[:, None]
    sample = np.arange(sample_count)[None, :]
    angles = 2.0 * math.pi / sample_count * (wave * sample % sample_count)
    table = np.concatenate([np.cos(angles), -np.sin(angles)], axis=0) / math.sqrt(freq_count)
    return table.astype(np.float32)


def cos_sin(angle):
    x = angle - math.pi / 4
    y = x * x
    c = jnp.float32(1.0)
    s = jnp.float32(1.0)
    for n in (5, 4, 3, 2, 1):
        c = 1.0 - y * (c * (1.0 / ((2 * n - 1) * (2 * n))))
        s = 1.0 - y * (s * (1.0 / ((2 * n) * (2 * n + 1))))
    s = s * x
    root = math.sqrt(0.5)
    return root * (c - s), root * (c + s)


def turn(a, b):
    return a[0] * b[0] - a[1] * b[1], a[0] * b[1] + a[1] * b[0]


def phasor_blocks(amplitude, arrival, freq_count, write):
    one = cos_sin(arrival * (2.0 * math.pi / (2 * freq_count)))
    one = (one[0], -one[1])
    powers = [None, one]
    for n in range(2, HALF + 1):
        powers.append(turn(powers[n // 2], powers[n - n // 2]))
    step = turn(powers[HALF], powers[HALF])
    centre = (amplitude * powers[HALF][0], amplitude * powers[HALF][1])
    for k in range(HALF, freq_count, 2 * HALF):
        for n in range(1, HALF + 1):
            cc, ss = centre[0] * powers[n][0], centre[1] * powers[n][1]
            cs, sc = centre[0] * powers[n][1], centre[1] * powers[n][0]
            upper = (cc - ss, sc + cs) if n < HALF else centre
            write(k, n, ((cc + ss, sc - cs), upper))
        if k + 2 * HALF < freq_count:
            centre = turn(centre, step)


def frequency_order(block):
    order = []
    for k in range(block * BLOCK + HALF, (block + 1) * BLOCK, 2 * HALF):
        for n in range(1, HALF + 1):
            order += [k - n, k + n if n < HALF else k]
    return order


def make_phasors(amplitude, arrival, freq_count, phasor):
    rows, points = amplitude.shape
    lanes = 4 * BLOCK
    for start in range(0, points, lanes):

        def write(k, n, values):
            row = (k - HALF + 2 * (n - 1)) * rows
            for part in range(2):
                both = jnp.concatenate([values[0][part], values[1][part]], axis=0)
                at = part * points + start
                phasor[row : row + 2 * rows, at : at + lanes] = both.astype(jnp.bfloat16)

        cut = slice(start, start + lanes)
        phasor_blocks(amplitude[:, cut], arrival[:, cut], freq_count, write)


def split(value):
    high = value.astype(jnp.bfloat16)
    return high, (value - high.astype(jnp.float32)).astype(jnp.bfloat16)


def block_spectrum(tile, block, rows, green, phasor, spectrum):
    lanes = 4 * BLOCK
    lane = lax.broadcasted_iota(jnp.int32, (rows, lanes), 1) % BLOCK
    own = pl.ds(block * BLOCK, BLOCK)
    real = [green[tile, c, own, :] for c in (0, 1, 2, 2)]
    imag = [green[tile, c, own, :] for c in (3, 4, 5, 5)]
    weights = jnp.concatenate(
        [
            jnp.concatenate(real + imag, axis=0),
            jnp.concatenate([-g for g in imag] + real, axis=0),
        ],
        axis=1,
    )
    left = phasor[block * BLOCK * rows : (block + 1) * BLOCK * rows, :]
    product = lax.dot_general(
        left, weights, (((1,), (1,)), ((), ())), preferred_element_type=jnp.float32
    )
    picked = [None] * 2
    for place, k in enumerate(frequency_order(block)):
        here = lane == k % BLOCK
        for part in range(2):
            piece = product[place * rows : (place + 1) * rows, part * lanes : (part + 1) * lanes]
            picked[part] = piece if place == 0 else jnp.where(here, piece, picked[part])
    real_high, real_low = split(picked[0])
    imag_high, imag_low = split(picked[1])
    target = pl.ds(pl.multiple_of(tile * 2 * rows, 2 * rows), 2 * rows)
    at = 2 * block * lanes
    spectrum[target, at : at + lanes] = jnp.concatenate([real_high, real_low], axis=0)
    spectrum[target, at + lanes : at + 2 * lanes] = jnp.concatenate([imag_high, imag_low], axis=0)


def membership(ids, count, rupture, owner, row_count, rupture_total):
    tile_total = ids.shape[1]
    wide = row_count * rupture_total
    column = lax.broadcasted_iota(jnp.int32, (row_count, wide), 1)
    slot = lax.broadcasted_iota(jnp.int32, (row_count, 1), 0)
    pieces = []
    for tile in range(tile_total):
        place = owner[rupture[tile]] * row_count
        target = jnp.where(slot < count[tile], ids[:, tile : tile + 1] + place, -1)
        pieces += [(column == target).astype(jnp.float32)] * 2
    return jnp.concatenate(pieces, axis=0).T.astype(jnp.bfloat16)


def route_rows(member, value):
    return jnp.dot(member, value, preferred_element_type=jnp.float32)


def component_rows(total, c, freq_count):
    parts = []
    for part in range(2):
        for block in range(freq_count // BLOCK):
            at = ((2 * block + part) * 3 + c) * BLOCK
            parts.append(total[:, at : at + BLOCK])
    return jnp.concatenate(parts, axis=1)


def kernel(
    sites, devices,
    ids_hbm, count_hbm, rupture_hbm, owner_hbm, slip_hbm, time_hbm, green_hbm, out,
    ids, count, rupture, owner, slip, time, green,
    maps, phasors, spectrum, member, partial, landed,
    small_sems, green_sems, map_send, map_recv, sum_send, sum_recv,
):
    tile_total, rows, local_points = slip.shape
    freq_count = green.shape[2]
    me = lax.axis_index("site")
    mine = lax.axis_index("fault")
    barrier = pltpu.get_barrier_semaphore()

    def greet_site(step, carry):
        peer = lax.rem(me + step, sites)
        pl.semaphore_signal(barrier, inc=1, device_id={"site": peer}, device_id_type=MESH)
        return carry

    def greet_fault(step, carry):
        peer = lax.rem(mine + step, devices)
        pl.semaphore_signal(barrier, inc=1, device_id={"fault": peer}, device_id_type=MESH)
        return carry

    lax.fori_loop(1, sites, greet_site, 0)
    lax.fori_loop(1, devices, greet_fault, 0)
    pairs = (
        (slip_hbm, slip), (time_hbm, time), (ids_hbm, ids), (count_hbm, count),
        (rupture_hbm, rupture), (owner_hbm, owner),
    )
    small = [pltpu.make_async_copy(a, b, small_sems.at[i]) for i, (a, b) in enumerate(pairs)]
    for copy in small:
        copy.start()
    for tile in range(tile_total):
        pltpu.make_async_copy(green_hbm.at[tile], green.at[tile], green_sems.at[tile]).start()
    for copy in small[:2]:
        copy.wait()
    maps[me] = jnp.concatenate([slip[...].astype(jnp.float32), time[...]], axis=2)
    pl.semaphore_wait(barrier, sites + devices - 2)

    chunk = tile_total // CHUNKS

    def map_copy(part, step):
        tiles = pl.ds(part * chunk, chunk)
        return pltpu.make_async_remote_copy(
            src_ref=maps.at[me, tiles],
            dst_ref=maps.at[me, tiles],
            send_sem=map_send.at[part, step],
            recv_sem=map_recv.at[part, me],
            device_id={"site": lax.rem(me + step, sites)},
            device_id_type=MESH,
        )

    def map_arrival(part, step):
        source = lax.rem(me + step, sites)
        tiles = pl.ds(part * chunk, chunk)
        return pltpu.make_async_remote_copy(
            src_ref=maps.at[source, tiles],
            dst_ref=maps.at[source, tiles],
            send_sem=map_send.at[part, step],
            recv_sem=map_recv.at[part, source],
            device_id={"site": source},
            device_id_type=MESH,
        )

    def over(first, last, body):
        lax.fori_loop(first, last, lambda step, carry: (body(step), carry)[1], 0)

    def send(part):
        over(1, sites, lambda step: map_copy(part, step).start())

    over(0, AHEAD, send)
    for copy in small[2:]:
        copy.wait()
    member[...] = membership(ids, count, rupture, owner, rows, owner.shape[0])

    def compute(part):
        over(1, sites, lambda step: map_arrival(part, step).wait_recv())

        @pl.when(part + AHEAD < CHUNKS)
        def _():
            send(part + AHEAD)


        def group(index):
            first = part * chunk + index * len(phasors)
            for at, phasor in enumerate(phasors):
                tile = first + at
                pltpu.make_async_copy(green_hbm.at[tile], green.at[tile], green_sems.at[tile]).wait()
            for at, phasor in enumerate(phasors):
                tile = first + at
                blocks = [maps[site, tile] for site in range(sites)]
                amplitude = jnp.concatenate([b[:, :local_points] for b in blocks], axis=1)
                arrival = jnp.concatenate([b[:, local_points:] for b in blocks], axis=1)
                make_phasors(amplitude, arrival, freq_count, phasor)
                for block in range(freq_count // BLOCK):
                    block_spectrum(tile, block, rows, green, phasor, spectrum)

        over(0, chunk // len(phasors), group)

    over(0, CHUNKS, compute)
    routed = route_rows(member[...], spectrum[...])
    lanes = 4 * BLOCK
    routed = jnp.concatenate(
        [routed[:, at : at + 3 * BLOCK] for at in range(0, routed.shape[1], lanes)], axis=1
    )
    height = routed.shape[0] // devices
    for device in range(devices):
        partial[device] = routed[device * height : (device + 1) * height]

    def sum_copy(step):
        peer = lax.rem(mine + step, devices)
        return pltpu.make_async_remote_copy(
            src_ref=partial.at[peer],
            dst_ref=landed.at[mine],
            send_sem=sum_send.at[step],
            recv_sem=sum_recv.at[mine],
            device_id={"fault": peer},
            device_id_type=MESH,
        )

    def sum_arrival(step):
        source = lax.rem(mine + step, devices)
        return pltpu.make_async_remote_copy(
            src_ref=partial.at[source],
            dst_ref=landed.at[source],
            send_sem=sum_send.at[step],
            recv_sem=sum_recv.at[source],
            device_id={"fault": source},
            device_id_type=MESH,
        )

    over(1, devices, lambda step: sum_copy(step).start())
    total = partial[mine]
    for step in range(1, devices):
        sum_arrival(step).wait_recv()
        total = total + landed[lax.rem(mine + step, devices)]
    for c in range(3):
        found = component_rows(total, c, freq_count)
        for row in range(height):
            out[3 * row + c : 3 * row + c + 1, :] = found[row : row + 1]
    over(0, CHUNKS, lambda part: over(1, sites, lambda step: map_copy(part, step).wait_send()))
    over(1, devices, lambda step: sum_copy(step).wait_send())


def per_device(
    sites, devices,
    green_tensor, slip_map, rupture_time, variation_ids, variation_count, tile_rupture, owner_slot,
):
    green = jnp.swapaxes(green_tensor[0], 1, 2)
    tile_total, _, freq_count, points = green.shape
    rows, local_points = slip_map.shape[1:]
    rupture_total = owner_slot.shape[0]
    width = 8 * freq_count
    height = rupture_total * rows // devices
    vmem = pl.BlockSpec(memory_space=pltpu.VMEM)
    anywhere = pl.BlockSpec(memory_space=pl.ANY)
    dma = pltpu.SemaphoreType.DMA
    owned = pl.pallas_call(
        functools.partial(kernel, sites, devices),
        out_shape=jax.ShapeDtypeStruct((height * 3, 2 * freq_count), jnp.float32),
        in_specs=[anywhere] * 7,
        out_specs=vmem,
        scratch_shapes=[
            pltpu.VMEM((rows, tile_total), jnp.int32),
            pltpu.SMEM((tile_total,), jnp.int32),
            pltpu.SMEM((tile_total,), jnp.int32),
            pltpu.SMEM((rupture_total,), jnp.int32),
            pltpu.VMEM(slip_map.shape, slip_map.dtype),
            pltpu.VMEM(rupture_time.shape, jnp.float32),
            pltpu.VMEM(green.shape, jnp.bfloat16),
            pltpu.VMEM((sites, tile_total, rows, 2 * local_points), jnp.float32),
            [pltpu.VMEM((freq_count * rows, 2 * points), jnp.bfloat16)] * UNROLL,
            pltpu.VMEM((tile_total * 2 * rows, width), jnp.bfloat16),
            pltpu.VMEM((rupture_total * rows, tile_total * 2 * rows), jnp.bfloat16),
            pltpu.VMEM((devices, height, 6 * freq_count), jnp.float32),
            pltpu.VMEM((devices, height, 6 * freq_count), jnp.float32),
            dma((6,)),
            dma((tile_total,)),
            dma((CHUNKS, sites)),
            dma((CHUNKS, sites)),
            dma((devices,)),
            dma((devices,)),
        ],
        compiler_params=pltpu.CompilerParams(
            collective_id=0, has_side_effects=True, vmem_limit_bytes=60 * 1024 * 1024
        ),
        cost_estimate=pl.CostEstimate(flops=2 * 10**9, bytes_accessed=5 * 10**6, transcendentals=0),
    )(
        variation_ids.T, variation_count, tile_rupture, owner_slot,
        slip_map, rupture_time, green,
    )
    seismic = jnp.dot(
        owned,
        inverse_table(freq_count),
        precision=lax.Precision.HIGHEST,
        preferred_element_type=jnp.float32,
    )
    return seismic.reshape(rupture_total // devices, rows, 1, 3, 2 * freq_count)


def solution(mesh):
    placed = (
        P("site", "fault", None, None, None),
        P("fault", None, "site"),
        P("fault", None, "site"),
        P("fault", None),
        P("fault"),
        P("fault"),
        P(),
    )
    return jax.shard_map(
        functools.partial(per_device, mesh.shape["site"], mesh.shape["fault"]),
        mesh=mesh,
        in_specs=placed,
        out_specs=P("fault", None, "site", None, None),
        check_vma=False,
    )
```

```python
import functools
import math

import jax
import jax.numpy as jnp
import numpy as np
from jax import lax
from jax.experimental import pallas as pl
from jax.experimental.pallas import tpu as pltpu
from jax.sharding import PartitionSpec as P

BLOCK = 32
HALF = 8
CHUNK = 2
MESH = pl.DeviceIdType.MESH


def inverse_table(freq_count):
    sample_count = 2 * freq_count
    wave = np.arange(freq_count)[:, None]
    sample = np.arange(sample_count)[None, :]
    angles = 2.0 * math.pi / sample_count * (wave * sample % sample_count)
    table = np.concatenate([np.cos(angles), -np.sin(angles)], axis=0) / math.sqrt(freq_count)
    return table.astype(np.float32)


def cos_sin(angle):
    x = angle - math.pi / 4
    y = x * x
    c = jnp.float32(1.0)
    s = jnp.float32(1.0)
    for n in (5, 4, 3, 2, 1):
        c = 1.0 - y * (c * (1.0 / ((2 * n - 1) * (2 * n))))
        s = 1.0 - y * (s * (1.0 / ((2 * n) * (2 * n + 1))))
    s = s * x
    root = math.sqrt(0.5)
    return root * (c - s), root * (c + s)


def turn(a, b):
    return a[0] * b[0] - a[1] * b[1], a[0] * b[1] + a[1] * b[0]


def phasor_blocks(amplitude, arrival, freq_count, write):
    one = cos_sin(arrival * (2.0 * math.pi / (2 * freq_count)))
    one = (one[0], -one[1])
    powers = [None, one]
    for n in range(2, HALF + 1):
        powers.append(turn(powers[n // 2], powers[n - n // 2]))
    step = turn(powers[HALF], powers[HALF])
    centre = (amplitude * powers[HALF][0], amplitude * powers[HALF][1])
    for k in range(HALF, freq_count, 2 * HALF):
        for n in range(1, HALF + 1):
            cc, ss = centre[0] * powers[n][0], centre[1] * powers[n][1]
            cs, sc = centre[0] * powers[n][1], centre[1] * powers[n][0]
            upper = (cc - ss, sc + cs) if n < HALF else centre
            write(k, n, ((cc + ss, sc - cs), upper))
        if k + 2 * HALF < freq_count:
            centre = turn(centre, step)
        yield


def frequency_order(block):
    order = []
    for k in range(block * BLOCK + HALF, (block + 1) * BLOCK, 2 * HALF):
        for n in range(1, HALF + 1):
            order += [k - n, k + n if n < HALF else k]
    return order


def make_phasors(amplitude, arrival, freq_count, phasor):
    rows, points = amplitude.shape
    lanes = 4 * BLOCK
    for start in range(0, points, lanes):

        def write(k, n, values):
            row = (k - HALF + 2 * (n - 1)) * rows
            for part in range(2):
                both = jnp.concatenate([values[0][part], values[1][part]], axis=0)
                at = part * points + start
                phasor[row : row + 2 * rows, at : at + lanes] = both.astype(jnp.bfloat16)

        cut = slice(start, start + lanes)
        yield from phasor_blocks(amplitude[:, cut], arrival[:, cut], freq_count, write)


def split(value):
    high = value.astype(jnp.bfloat16)
    return high, (value - high.astype(jnp.float32)).astype(jnp.bfloat16)


def block_spectrum(tile, block, rows, green, phasor, spectrum):
    lanes = 4 * BLOCK
    lane = lax.broadcasted_iota(jnp.int32, (rows, lanes), 1) % BLOCK
    own = pl.ds(block * BLOCK, BLOCK)
    real = [green[tile, c, own, :] for c in (0, 1, 2, 2)]
    imag = [green[tile, c, own, :] for c in (3, 4, 5, 5)]
    weights = jnp.concatenate(
        [
            jnp.concatenate(real + imag, axis=0),
            jnp.concatenate([-g for g in imag] + real, axis=0),
        ],
        axis=1,
    )
    left = phasor[block * BLOCK * rows : (block + 1) * BLOCK * rows, :]
    product = lax.dot_general(
        left, weights, (((1,), (1,)), ((), ())), preferred_element_type=jnp.float32
    )
    picked = [None] * 2
    for place, k in enumerate(frequency_order(block)):
        here = lane == k % BLOCK
        for part in range(2):
            piece = product[place * rows : (place + 1) * rows, part * lanes : (part + 1) * lanes]
            picked[part] = piece if place == 0 else jnp.where(here, piece, picked[part])
    real_high, real_low = split(picked[0])
    imag_high, imag_low = split(picked[1])
    target = pl.ds(pl.multiple_of(tile * 2 * rows, 2 * rows), 2 * rows)
    at = 2 * block * lanes
    spectrum[target, at : at + lanes] = jnp.concatenate([real_high, real_low], axis=0)
    spectrum[target, at + lanes : at + 2 * lanes] = jnp.concatenate([imag_high, imag_low], axis=0)


def membership(ids, count, rupture, owner, row_count, rupture_total):
    tile_total = ids.shape[1]
    wide = row_count * rupture_total
    column = lax.broadcasted_iota(jnp.int32, (row_count, wide), 1)
    slot = lax.broadcasted_iota(jnp.int32, (row_count, 1), 0)
    pieces = []
    for tile in range(tile_total):
        place = owner[rupture[tile]] * row_count
        target = jnp.where(slot < count[tile], ids[:, tile : tile + 1] + place, -1)
        pieces += [(column == target).astype(jnp.float32)] * 2
    return jnp.concatenate(pieces, axis=0).T.astype(jnp.bfloat16)


def route_rows(member, value):
    return jnp.dot(member, value, preferred_element_type=jnp.float32)


def inverse(total, table, freq_count):
    rows = []
    for c in range(3):
        parts = []
        for part in range(2):
            for block in range(freq_count // BLOCK):
                at = ((2 * block + part) * 3 + c) * BLOCK
                parts.append(total[:, at : at + BLOCK])
        rows.append(jnp.concatenate(parts, axis=1))
    return jnp.dot(
        jnp.concatenate(rows, axis=0),
        table,
        precision=lax.Precision.HIGHEST,
        preferred_element_type=jnp.float32,
    )


def kernel(
    sites, devices,
    ids_hbm, count_hbm, rupture_hbm, owner_hbm, slip_hbm, time_hbm, table_hbm, green_hbm, out,
    ids, count, rupture, owner, slip, time, table, green,
    maps, phasors, spectrum, member, partial, landed,
    small_sems, green_sems, map_send, map_recv, sum_send, sum_recv,
):
    tile_total, rows, local_points = slip.shape
    freq_count = green.shape[2]
    me = lax.axis_index("site")
    mine = lax.axis_index("fault")
    barrier = pltpu.get_barrier_semaphore()

    def greet_site(step, carry):
        peer = lax.rem(me + step, sites)
        pl.semaphore_signal(barrier, inc=1, device_id={"site": peer}, device_id_type=MESH)
        return carry

    def greet_fault(step, carry):
        peer = lax.rem(mine + step, devices)
        pl.semaphore_signal(barrier, inc=1, device_id={"fault": peer}, device_id_type=MESH)
        return carry

    lax.fori_loop(1, sites, greet_site, 0)
    lax.fori_loop(1, devices, greet_fault, 0)
    pairs = (
        (slip_hbm, slip), (time_hbm, time), (ids_hbm, ids), (count_hbm, count),
        (rupture_hbm, rupture), (owner_hbm, owner), (table_hbm, table),
    )
    small = [pltpu.make_async_copy(a, b, small_sems.at[i]) for i, (a, b) in enumerate(pairs)]
    for copy in small[:-1]:
        copy.start()
    for tile in range(tile_total):
        pltpu.make_async_copy(green_hbm.at[tile], green.at[tile], green_sems.at[tile]).start()
    small[-1].start()
    for copy in small[:2]:
        copy.wait()
    maps[me] = jnp.concatenate([slip[...].astype(jnp.float32), time[...]], axis=2)
    pl.semaphore_wait(barrier, sites + devices - 2)

    chunk = CHUNK
    chunks = tile_total // CHUNK

    def map_copy(part, step):
        tiles = pl.ds(part * chunk, chunk)
        return pltpu.make_async_remote_copy(
            src_ref=maps.at[me, tiles],
            dst_ref=maps.at[me, tiles],
            send_sem=map_send.at[part, step],
            recv_sem=map_recv.at[part, me],
            device_id={"site": lax.rem(me + step, sites)},
            device_id_type=MESH,
        )

    def map_arrival(part, step):
        source = lax.rem(me + step, sites)
        tiles = pl.ds(part * chunk, chunk)
        return pltpu.make_async_remote_copy(
            src_ref=maps.at[source, tiles],
            dst_ref=maps.at[source, tiles],
            send_sem=map_send.at[part, step],
            recv_sem=map_recv.at[part, source],
            device_id={"site": source},
            device_id_type=MESH,
        )

    def over(first, last, body):
        lax.fori_loop(first, last, lambda step, carry: (body(step), carry)[1], 0)

    over(0, chunks, lambda part: over(1, sites, lambda step: map_copy(part, step).start()))
    for copy in small[2:-1]:
        copy.wait()
    member[...] = membership(ids, count, rupture, owner, rows, owner.shape[0])

    def arrive(part):
        over(1, sites, lambda step: map_arrival(part, step).wait_recv())

    def phasor_steps(tile, phasor):
        blocks = [maps[site, tile] for site in range(sites)]
        amplitude = jnp.concatenate([b[:, :local_points] for b in blocks], axis=1)
        arrival = jnp.concatenate([b[:, local_points:] for b in blocks], axis=1)
        return make_phasors(amplitude, arrival, freq_count, phasor)

    def dots_beside(tile, phasor, steps):
        block_count = freq_count // BLOCK
        share = -(-(2 * freq_count // (2 * HALF)) // block_count)
        for block in range(block_count):
            block_spectrum(tile, block, rows, green, phasor, spectrum)
            for _ in range(share):
                next(steps, None)
        for _ in steps:
            pass

    def green_arrive(tile):
        pltpu.make_async_copy(green_hbm.at[tile], green.at[tile], green_sems.at[tile]).wait()

    def pair(index):
        first = index * chunk
        arrive(index + 1)
        green_arrive(first)
        green_arrive(first + 1)
        dots_beside(first, phasors[0], phasor_steps(first + 1, phasors[1]))
        dots_beside(first + 1, phasors[1], phasor_steps(first + 2, phasors[0]))

    arrive(0)
    for _ in phasor_steps(0, phasors[0]):
        pass
    over(0, chunks - 1, pair)
    last = tile_total - 2
    green_arrive(last)
    green_arrive(last + 1)
    dots_beside(last, phasors[0], phasor_steps(last + 1, phasors[1]))
    dots_beside(last + 1, phasors[1], iter(()))
    routed = route_rows(member[...], spectrum[...])
    lanes = 4 * BLOCK
    routed = jnp.concatenate(
        [routed[:, at : at + 3 * BLOCK] for at in range(0, routed.shape[1], lanes)], axis=1
    )
    height = routed.shape[0] // devices
    for device in range(devices):
        partial[device] = routed[device * height : (device + 1) * height]

    def sum_copy(step):
        peer = lax.rem(mine + step, devices)
        return pltpu.make_async_remote_copy(
            src_ref=partial.at[peer],
            dst_ref=landed.at[mine],
            send_sem=sum_send.at[step],
            recv_sem=sum_recv.at[mine],
            device_id={"fault": peer},
            device_id_type=MESH,
        )

    def sum_arrival(step):
        source = lax.rem(mine + step, devices)
        return pltpu.make_async_remote_copy(
            src_ref=partial.at[source],
            dst_ref=landed.at[source],
            send_sem=sum_send.at[step],
            recv_sem=sum_recv.at[source],
            device_id={"fault": source},
            device_id_type=MESH,
        )

    over(1, devices, lambda step: sum_copy(step).start())
    small[-1].wait()
    total = partial[mine]
    for step in range(1, devices):
        sum_arrival(step).wait_recv()
        total = total + landed[lax.rem(mine + step, devices)]
    seismic = inverse(total, table[...], freq_count)
    for c in range(3):
        for row in range(height):
            at = c * height + row
            out[row, c] = seismic[at : at + 1]
    over(0, chunks, lambda part: over(1, sites, lambda step: map_copy(part, step).wait_send()))
    over(1, devices, lambda step: sum_copy(step).wait_send())


def per_device(
    sites, devices,
    green_tensor, slip_map, rupture_time, variation_ids, variation_count, tile_rupture, owner_slot,
):
    green = jnp.swapaxes(green_tensor[0], 1, 2)
    tile_total, _, freq_count, points = green.shape
    rows, local_points = slip_map.shape[1:]
    rupture_total = owner_slot.shape[0]
    width = 8 * freq_count
    height = rupture_total * rows // devices
    vmem = pl.BlockSpec(memory_space=pltpu.VMEM)
    anywhere = pl.BlockSpec(memory_space=pl.ANY)
    dma = pltpu.SemaphoreType.DMA
    seismic = pl.pallas_call(
        functools.partial(kernel, sites, devices),
        out_shape=jax.ShapeDtypeStruct((height, 3, 1, 2 * freq_count), jnp.float32),
        in_specs=[anywhere] * 8,
        out_specs=vmem,
        scratch_shapes=[
            pltpu.VMEM((rows, tile_total), jnp.int32),
            pltpu.SMEM((tile_total,), jnp.int32),
            pltpu.SMEM((tile_total,), jnp.int32),
            pltpu.SMEM((rupture_total,), jnp.int32),
            pltpu.VMEM(slip_map.shape, slip_map.dtype),
            pltpu.VMEM(rupture_time.shape, jnp.float32),
            pltpu.VMEM((2 * freq_count, 2 * freq_count), jnp.float32),
            pltpu.VMEM(green.shape, jnp.bfloat16),
            pltpu.VMEM((sites, tile_total, rows, 2 * local_points), jnp.float32),
            [pltpu.VMEM((freq_count * rows, 2 * points), jnp.bfloat16)] * 2,
            pltpu.VMEM((tile_total * 2 * rows, width), jnp.bfloat16),
            pltpu.VMEM((rupture_total * rows, tile_total * 2 * rows), jnp.bfloat16),
            pltpu.VMEM((devices, height, 6 * freq_count), jnp.float32),
            pltpu.VMEM((devices, height, 6 * freq_count), jnp.float32),
            dma((7,)),
            dma((tile_total,)),
            dma((tile_total // CHUNK, sites)),
            dma((tile_total // CHUNK, sites)),
            dma((devices,)),
            dma((devices,)),
        ],
        compiler_params=pltpu.CompilerParams(
            collective_id=0, has_side_effects=True, vmem_limit_bytes=60 * 1024 * 1024
        ),
        cost_estimate=pl.CostEstimate(flops=2 * 10**9, bytes_accessed=5 * 10**6, transcendentals=0),
    )(
        variation_ids.T, variation_count, tile_rupture, owner_slot,
        slip_map, rupture_time, inverse_table(freq_count), green,
    )
    seismic = seismic.reshape(rupture_total // devices, rows, 3, 1, 2 * freq_count)
    return jnp.swapaxes(seismic, 2, 3)


def solution(mesh):
    placed = (
        P("site", "fault", None, None, None),
        P("fault", None, "site"),
        P("fault", None, "site"),
        P("fault", None),
        P("fault"),
        P("fault"),
        P(),
    )
    return jax.shard_map(
        functools.partial(per_device, mesh.shape["site"], mesh.shape["fault"]),
        mesh=mesh,
        in_specs=placed,
        out_specs=P("fault", None, "site", None, None),
        check_vma=False,
    )
```

```python
import functools
import math

import jax
import jax.numpy as jnp
import numpy as np
from jax import lax
from jax.experimental import pallas as pl
from jax.experimental.pallas import tpu as pltpu
from jax.sharding import PartitionSpec as P

BLOCK = 32
HALF = 8
CHUNK = 2
MESH = pl.DeviceIdType.MESH


def inverse_table(freq_count):
    sample_count = 2 * freq_count
    wave = np.arange(freq_count)[:, None]
    sample = np.arange(sample_count)[None, :]
    angles = 2.0 * math.pi / sample_count * (wave * sample % sample_count)
    table = np.concatenate([np.cos(angles), -np.sin(angles)], axis=0) / math.sqrt(freq_count)
    return table.astype(np.float32)


def cos_sin(angle):
    x = angle - math.pi / 4
    y = x * x
    c = jnp.float32(1.0)
    s = jnp.float32(1.0)
    for n in (5, 4, 3, 2, 1):
        c = 1.0 - y * (c * (1.0 / ((2 * n - 1) * (2 * n))))
        s = 1.0 - y * (s * (1.0 / ((2 * n) * (2 * n + 1))))
    s = s * x
    root = math.sqrt(0.5)
    return root * (c - s), root * (c + s)


def turn(a, b):
    return a[0] * b[0] - a[1] * b[1], a[0] * b[1] + a[1] * b[0]


def phasor_blocks(amplitude, arrival, freq_count, write):
    one = cos_sin(arrival * (2.0 * math.pi / (2 * freq_count)))
    one = (one[0], -one[1])
    powers = [None, one]
    for n in range(2, HALF + 1):
        powers.append(turn(powers[n // 2], powers[n - n // 2]))
    step = turn(powers[HALF], powers[HALF])
    centre = (amplitude * powers[HALF][0], amplitude * powers[HALF][1])
    for k in range(HALF, freq_count, 2 * HALF):
        for n in range(1, HALF + 1):
            cc, ss = centre[0] * powers[n][0], centre[1] * powers[n][1]
            cs, sc = centre[0] * powers[n][1], centre[1] * powers[n][0]
            upper = (cc - ss, sc + cs) if n < HALF else centre
            write(k, n, ((cc + ss, sc - cs), upper))
        if k + 2 * HALF < freq_count:
            centre = turn(centre, step)
        yield


def frequency_order(block):
    order = []
    for k in range(block * BLOCK + HALF, (block + 1) * BLOCK, 2 * HALF):
        for n in range(1, HALF + 1):
            order += [k - n, k + n if n < HALF else k]
    return order


def make_phasors(amplitude, arrival, freq_count, phasor):
    rows, points = amplitude.shape
    lanes = 4 * BLOCK
    for start in range(0, points, lanes):

        def write(k, n, values):
            row = (k - HALF + 2 * (n - 1)) * rows
            for part in range(2):
                both = jnp.concatenate([values[0][part], values[1][part]], axis=0)
                at = part * points + start
                phasor[row : row + 2 * rows, at : at + lanes] = both.astype(jnp.bfloat16)

        cut = slice(start, start + lanes)
        yield from phasor_blocks(amplitude[:, cut], arrival[:, cut], freq_count, write)


def split(value):
    high = value.astype(jnp.bfloat16)
    return high, (value - high.astype(jnp.float32)).astype(jnp.bfloat16)


def block_spectrum(tile, block, rows, green, phasor, spectrum):
    lanes = 4 * BLOCK
    lane = lax.broadcasted_iota(jnp.int32, (rows, lanes), 1) % BLOCK
    own = pl.ds(block * BLOCK, BLOCK)
    real = [green[tile, c, own, :] for c in (0, 1, 2, 2)]
    imag = [green[tile, c, own, :] for c in (3, 4, 5, 5)]
    weights = jnp.concatenate(
        [
            jnp.concatenate(real + imag, axis=0),
            jnp.concatenate([-g for g in imag] + real, axis=0),
        ],
        axis=1,
    )
    left = phasor[block * BLOCK * rows : (block + 1) * BLOCK * rows, :]
    product = lax.dot_general(
        left, weights, (((1,), (1,)), ((), ())), preferred_element_type=jnp.float32
    )
    picked = [None] * 2
    for place, k in enumerate(frequency_order(block)):
        here = lane == k % BLOCK
        for part in range(2):
            piece = product[place * rows : (place + 1) * rows, part * lanes : (part + 1) * lanes]
            picked[part] = piece if place == 0 else jnp.where(here, piece, picked[part])
    real_high, real_low = split(picked[0])
    imag_high, imag_low = split(picked[1])
    target = pl.ds(pl.multiple_of(tile * 2 * rows, 2 * rows), 2 * rows)
    at = 2 * block * lanes
    spectrum[target, at : at + lanes] = jnp.concatenate([real_high, real_low], axis=0)
    spectrum[target, at + lanes : at + 2 * lanes] = jnp.concatenate([imag_high, imag_low], axis=0)


def membership(ids, count, rupture, owner, row_count, rupture_total):
    tile_total = ids.shape[1]
    wide = row_count * rupture_total
    column = lax.broadcasted_iota(jnp.int32, (row_count, wide), 1)
    slot = lax.broadcasted_iota(jnp.int32, (row_count, 1), 0)
    pieces = []
    for tile in range(tile_total):
        place = owner[rupture[tile]] * row_count
        target = jnp.where(slot < count[tile], ids[:, tile : tile + 1] + place, -1)
        pieces += [(column == target).astype(jnp.float32)] * 2
    return jnp.concatenate(pieces, axis=0).T.astype(jnp.bfloat16)


def route_rows(member, value):
    return jnp.dot(member, value, preferred_element_type=jnp.float32)


def inverse(total, table, freq_count):
    rows = []
    for c in range(3):
        parts = []
        for part in range(2):
            for block in range(freq_count // BLOCK):
                at = ((2 * block + part) * 3 + c) * BLOCK
                parts.append(total[:, at : at + BLOCK])
        rows.append(jnp.concatenate(parts, axis=1))
    return jnp.dot(
        jnp.concatenate(rows, axis=0),
        table,
        precision=lax.Precision.HIGHEST,
        preferred_element_type=jnp.float32,
    )


def kernel(
    sites, devices,
    ids_hbm, count_hbm, rupture_hbm, owner_hbm, slip_hbm, time_hbm, table_hbm, green_hbm, out,
    ids, count, rupture, owner, slip, time, table, green,
    maps, phasors, spectrum, member, partial, landed,
    small_sems, green_sems, map_send, map_recv, sum_send, sum_recv,
):
    tile_total, rows, local_points = slip.shape
    freq_count = green.shape[2]
    me = lax.axis_index("site")
    mine = lax.axis_index("fault")
    barrier = pltpu.get_barrier_semaphore()

    def greet_site(step, carry):
        peer = lax.rem(me + step, sites)
        pl.semaphore_signal(barrier, inc=1, device_id={"site": peer}, device_id_type=MESH)
        return carry

    def greet_fault(step, carry):
        peer = lax.rem(mine + step, devices)
        pl.semaphore_signal(barrier, inc=1, device_id={"fault": peer}, device_id_type=MESH)
        return carry

    lax.fori_loop(1, sites, greet_site, 0)
    lax.fori_loop(1, devices, greet_fault, 0)
    pairs = (
        (slip_hbm, slip), (time_hbm, time), (ids_hbm, ids), (count_hbm, count),
        (rupture_hbm, rupture), (owner_hbm, owner), (table_hbm, table),
    )
    small = [pltpu.make_async_copy(a, b, small_sems.at[i]) for i, (a, b) in enumerate(pairs)]
    for copy in small[:-1]:
        copy.start()
    for tile in range(tile_total):
        pltpu.make_async_copy(green_hbm.at[tile], green.at[tile], green_sems.at[tile]).start()
    small[-1].start()
    for copy in small[:2]:
        copy.wait()
    maps[me] = jnp.concatenate([slip[...].astype(jnp.float32), time[...]], axis=2)
    pl.semaphore_wait(barrier, sites + devices - 2)

    chunk = CHUNK
    chunks = tile_total // CHUNK

    def map_copy(part, step):
        tiles = pl.ds(part * chunk, chunk)
        return pltpu.make_async_remote_copy(
            src_ref=maps.at[me, tiles],
            dst_ref=maps.at[me, tiles],
            send_sem=map_send.at[part, step],
            recv_sem=map_recv.at[part, me],
            device_id={"site": lax.rem(me + step, sites)},
            device_id_type=MESH,
        )

    def map_arrival(part, step):
        source = lax.rem(me + step, sites)
        tiles = pl.ds(part * chunk, chunk)
        return pltpu.make_async_remote_copy(
            src_ref=maps.at[source, tiles],
            dst_ref=maps.at[source, tiles],
            send_sem=map_send.at[part, step],
            recv_sem=map_recv.at[part, source],
            device_id={"site": source},
            device_id_type=MESH,
        )

    def over(first, last, body):
        lax.fori_loop(first, last, lambda step, carry: (body(step), carry)[1], 0)

    over(0, chunks, lambda part: over(1, sites, lambda step: map_copy(part, step).start()))
    for copy in small[2:-1]:
        copy.wait()
    member[...] = membership(ids, count, rupture, owner, rows, owner.shape[0])

    def arrive(part):
        over(1, sites, lambda step: map_arrival(part, step).wait_recv())

    def phasor_steps(tile, phasor):
        blocks = [maps[site, tile] for site in range(sites)]
        amplitude = jnp.concatenate([b[:, :local_points] for b in blocks], axis=1)
        arrival = jnp.concatenate([b[:, local_points:] for b in blocks], axis=1)
        return make_phasors(amplitude, arrival, freq_count, phasor)

    def dots_beside(tile, phasor, steps):
        block_count = freq_count // BLOCK
        share = -(-(2 * freq_count // (2 * HALF)) // block_count)
        for block in range(block_count):
            block_spectrum(tile, block, rows, green, phasor, spectrum)
            for _ in range(share):
                next(steps, None)
        for _ in steps:
            pass

    def green_arrive(tile):
        pltpu.make_async_copy(green_hbm.at[tile], green.at[tile], green_sems.at[tile]).wait()

    def pair(index):
        first = index * chunk
        arrive(index + 1)
        green_arrive(first)
        green_arrive(first + 1)
        dots_beside(first, phasors[0], phasor_steps(first + 1, phasors[1]))
        dots_beside(first + 1, phasors[1], phasor_steps(first + 2, phasors[0]))

    arrive(0)
    for _ in phasor_steps(0, phasors[0]):
        pass
    over(0, chunks - 1, pair)
    last = tile_total - 2
    green_arrive(last)
    green_arrive(last + 1)
    dots_beside(last, phasors[0], phasor_steps(last + 1, phasors[1]))
    dots_beside(last + 1, phasors[1], iter(()))
    routed = route_rows(member[...], spectrum[...])
    lanes = 4 * BLOCK
    routed = jnp.concatenate(
        [routed[:, at : at + 3 * BLOCK] for at in range(0, routed.shape[1], lanes)], axis=1
    )
    height = routed.shape[0] // devices
    for device in range(devices):
        partial[device] = routed[device * height : (device + 1) * height]

    def sum_copy(step):
        peer = lax.rem(mine + step, devices)
        return pltpu.make_async_remote_copy(
            src_ref=partial.at[peer],
            dst_ref=landed.at[mine],
            send_sem=sum_send.at[step],
            recv_sem=sum_recv.at[mine],
            device_id={"fault": peer},
            device_id_type=MESH,
        )

    def sum_arrival(step):
        source = lax.rem(mine + step, devices)
        return pltpu.make_async_remote_copy(
            src_ref=partial.at[source],
            dst_ref=landed.at[source],
            send_sem=sum_send.at[step],
            recv_sem=sum_recv.at[source],
            device_id={"fault": source},
            device_id_type=MESH,
        )

    over(1, devices, lambda step: sum_copy(step).start())
    small[-1].wait()
    total = partial[mine]
    for step in range(1, devices):
        sum_arrival(step).wait_recv()
        total = total + landed[lax.rem(mine + step, devices)]
    seismic = inverse(total, table[...], freq_count)
    for c in range(3):
        for row in range(height):
            at = c * height + row
            out[row, c] = seismic[at : at + 1]
    over(0, chunks, lambda part: over(1, sites, lambda step: map_copy(part, step).wait_send()))
    over(1, devices, lambda step: sum_copy(step).wait_send())


def per_device(
    sites, devices,
    green_tensor, slip_map, rupture_time, variation_ids, variation_count, tile_rupture, owner_slot,
):
    green = jnp.swapaxes(green_tensor[0], 1, 2)
    tile_total, _, freq_count, points = green.shape
    rows, local_points = slip_map.shape[1:]
    rupture_total = owner_slot.shape[0]
    width = 8 * freq_count
    height = rupture_total * rows // devices
    vmem = pl.BlockSpec(memory_space=pltpu.VMEM)
    anywhere = pl.BlockSpec(memory_space=pl.ANY)
    dma = pltpu.SemaphoreType.DMA
    seismic = pl.pallas_call(
        functools.partial(kernel, sites, devices),
        out_shape=jax.ShapeDtypeStruct((height, 3, 1, 2 * freq_count), jnp.float32),
        in_specs=[anywhere] * 8,
        out_specs=vmem,
        scratch_shapes=[
            pltpu.VMEM((rows, tile_total), jnp.int32),
            pltpu.SMEM((tile_total,), jnp.int32),
            pltpu.SMEM((tile_total,), jnp.int32),
            pltpu.SMEM((rupture_total,), jnp.int32),
            pltpu.VMEM(slip_map.shape, slip_map.dtype),
            pltpu.VMEM(rupture_time.shape, jnp.float32),
            pltpu.VMEM((2 * freq_count, 2 * freq_count), jnp.float32),
            pltpu.VMEM(green.shape, jnp.bfloat16),
            pltpu.VMEM((sites, tile_total, rows, 2 * local_points), jnp.float32),
            [pltpu.VMEM((freq_count * rows, 2 * points), jnp.bfloat16)] * 2,
            pltpu.VMEM((tile_total * 2 * rows, width), jnp.bfloat16),
            pltpu.VMEM((rupture_total * rows, tile_total * 2 * rows), jnp.bfloat16),
            pltpu.VMEM((devices, height, 6 * freq_count), jnp.float32),
            pltpu.VMEM((devices, height, 6 * freq_count), jnp.float32),
            dma((7,)),
            dma((tile_total,)),
            dma((tile_total // CHUNK, sites)),
            dma((tile_total // CHUNK, sites)),
            dma((devices,)),
            dma((devices,)),
        ],
        compiler_params=pltpu.CompilerParams(
            collective_id=0, has_side_effects=True, vmem_limit_bytes=50 * 1024 * 1024
        ),
        cost_estimate=pl.CostEstimate(flops=2 * 10**9, bytes_accessed=5 * 10**6, transcendentals=0),
    )(
        variation_ids.T, variation_count, tile_rupture, owner_slot,
        slip_map, rupture_time, inverse_table(freq_count), green,
    )
    seismic = seismic.reshape(rupture_total // devices, rows, 3, 1, 2 * freq_count)
    return jnp.swapaxes(seismic, 2, 3)


def solution(mesh):
    placed = (
        P("site", "fault", None, None, None),
        P("fault", None, "site"),
        P("fault", None, "site"),
        P("fault", None),
        P("fault"),
        P("fault"),
        P(),
    )
    return jax.shard_map(
        functools.partial(per_device, mesh.shape["site"], mesh.shape["fault"]),
        mesh=mesh,
        in_specs=placed,
        out_specs=P("fault", None, "site", None, None),
        check_vma=False,
    )
```

```python
import functools
import math

import jax
import jax.numpy as jnp
import numpy as np
from jax import lax
from jax.experimental import pallas as pl
from jax.experimental.pallas import tpu as pltpu
from jax.sharding import PartitionSpec as P

BLOCK = 32
HALF = 8
CHUNK = 2
MESH = pl.DeviceIdType.MESH


def inverse_table(freq_count):
    sample_count = 2 * freq_count
    wave = np.arange(freq_count)[:, None]
    sample = np.arange(sample_count)[None, :]
    angles = 2.0 * math.pi / sample_count * (wave * sample % sample_count)
    table = np.concatenate([np.cos(angles), -np.sin(angles)], axis=0) / math.sqrt(freq_count)
    return table.astype(np.float32)


def cos_sin(angle):
    x = angle - math.pi / 4
    y = x * x
    c = jnp.float32(1.0)
    s = jnp.float32(1.0)
    for n in (5, 4, 3, 2, 1):
        c = 1.0 - y * (c * (1.0 / ((2 * n - 1) * (2 * n))))
        s = 1.0 - y * (s * (1.0 / ((2 * n) * (2 * n + 1))))
    s = s * x
    root = math.sqrt(0.5)
    return root * (c - s), root * (c + s)


def turn(a, b):
    return a[0] * b[0] - a[1] * b[1], a[0] * b[1] + a[1] * b[0]


def phasor_blocks(amplitude, arrival, freq_count, write):
    one = cos_sin(arrival * (2.0 * math.pi / (2 * freq_count)))
    one = (one[0], -one[1])
    powers = [None, one]
    for n in range(2, HALF + 1):
        powers.append(turn(powers[n // 2], powers[n - n // 2]))
    step = turn(powers[HALF], powers[HALF])
    centre = (amplitude * powers[HALF][0], amplitude * powers[HALF][1])
    for k in range(HALF, freq_count, 2 * HALF):
        for n in range(1, HALF + 1):
            cc, ss = centre[0] * powers[n][0], centre[1] * powers[n][1]
            cs, sc = centre[0] * powers[n][1], centre[1] * powers[n][0]
            upper = (cc - ss, sc + cs) if n < HALF else centre
            write(k, n, ((cc + ss, sc - cs), upper))
        if k + 2 * HALF < freq_count:
            centre = turn(centre, step)
        yield


def frequency_order(block):
    order = []
    for k in range(block * BLOCK + HALF, (block + 1) * BLOCK, 2 * HALF):
        for n in range(1, HALF + 1):
            order += [k - n, k + n if n < HALF else k]
    return order


def make_phasors(amplitude, arrival, freq_count, phasor):
    rows, points = amplitude.shape
    lanes = 4 * BLOCK
    for start in range(0, points, lanes):

        def write(k, n, values):
            row = (k - HALF + 2 * (n - 1)) * rows
            for part in range(2):
                both = jnp.concatenate([values[0][part], values[1][part]], axis=0)
                at = part * points + start
                phasor[row : row + 2 * rows, at : at + lanes] = both.astype(jnp.bfloat16)

        cut = slice(start, start + lanes)
        yield from phasor_blocks(amplitude[:, cut], arrival[:, cut], freq_count, write)


def split(value):
    high = value.astype(jnp.bfloat16)
    return high, (value - high.astype(jnp.float32)).astype(jnp.bfloat16)


def block_spectrum(tile, block, rows, green, phasor, spectrum):
    lanes = 4 * BLOCK
    lane = lax.broadcasted_iota(jnp.int32, (rows, lanes), 1) % BLOCK
    own = pl.ds(block * BLOCK, BLOCK)
    real = [green[tile, c, own, :] for c in (0, 1, 2, 2)]
    imag = [green[tile, c, own, :] for c in (3, 4, 5, 5)]
    weights = jnp.concatenate(
        [
            jnp.concatenate(real + imag, axis=0),
            jnp.concatenate([-g for g in imag] + real, axis=0),
        ],
        axis=1,
    )
    left = phasor[block * BLOCK * rows : (block + 1) * BLOCK * rows, :]
    product = lax.dot_general(
        left, weights, (((1,), (1,)), ((), ())), preferred_element_type=jnp.float32
    )
    picked = [None] * 2
    for place, k in enumerate(frequency_order(block)):
        here = lane == k % BLOCK
        for part in range(2):
            piece = product[place * rows : (place + 1) * rows, part * lanes : (part + 1) * lanes]
            picked[part] = piece if place == 0 else jnp.where(here, piece, picked[part])
    real_high, real_low = split(picked[0])
    imag_high, imag_low = split(picked[1])
    target = pl.ds(pl.multiple_of(tile * 2 * rows, 2 * rows), 2 * rows)
    at = 2 * block * lanes
    spectrum[target, at : at + lanes] = jnp.concatenate([real_high, real_low], axis=0)
    spectrum[target, at + lanes : at + 2 * lanes] = jnp.concatenate([imag_high, imag_low], axis=0)


def membership(ids, count, rupture, owner, row_count, rupture_total):
    tile_total = ids.shape[1]
    wide = row_count * rupture_total
    column = lax.broadcasted_iota(jnp.int32, (row_count, wide), 1)
    slot = lax.broadcasted_iota(jnp.int32, (row_count, 1), 0)
    pieces = []
    for tile in range(tile_total):
        place = owner[rupture[tile]] * row_count
        target = jnp.where(slot < count[tile], ids[:, tile : tile + 1] + place, -1)
        pieces += [(column == target).astype(jnp.float32)] * 2
    return jnp.concatenate(pieces, axis=0).T.astype(jnp.bfloat16)


def route_rows(member, value):
    return jnp.dot(member, value, preferred_element_type=jnp.float32)


def inverse(total, table, freq_count):
    rows = []
    for c in range(3):
        parts = []
        for part in range(2):
            for block in range(freq_count // BLOCK):
                at = ((2 * block + part) * 3 + c) * BLOCK
                parts.append(total[:, at : at + BLOCK])
        rows.append(jnp.concatenate(parts, axis=1))
    return jnp.dot(
        jnp.concatenate(rows, axis=0),
        table,
        precision=lax.Precision.HIGHEST,
        preferred_element_type=jnp.float32,
    )


def kernel(
    sites, devices,
    ids_hbm, count_hbm, rupture_hbm, owner_hbm, slip_hbm, time_hbm, table_hbm, green_hbm, out,
    ids, count, rupture, owner, slip, time, table, green,
    maps, phasors, spectrum, member, partial, landed,
    small_sems, green_sems, map_send, map_recv, sum_send, sum_recv,
):
    tile_total, rows, local_points = slip.shape
    freq_count = green.shape[2]
    me = lax.axis_index("site")
    mine = lax.axis_index("fault")
    barrier = pltpu.get_barrier_semaphore()

    def greet_site(step, carry):
        peer = lax.rem(me + step, sites)
        pl.semaphore_signal(barrier, inc=1, device_id={"site": peer}, device_id_type=MESH)
        return carry

    def greet_fault(step, carry):
        peer = lax.rem(mine + step, devices)
        pl.semaphore_signal(barrier, inc=1, device_id={"fault": peer}, device_id_type=MESH)
        return carry

    lax.fori_loop(1, sites, greet_site, 0)
    lax.fori_loop(1, devices, greet_fault, 0)
    pairs = (
        (slip_hbm, slip), (time_hbm, time), (ids_hbm, ids), (count_hbm, count),
        (rupture_hbm, rupture), (owner_hbm, owner), (table_hbm, table),
    )
    small = [pltpu.make_async_copy(a, b, small_sems.at[i]) for i, (a, b) in enumerate(pairs)]
    for copy in small[:-1]:
        copy.start()
    for copy in small[:2]:
        copy.wait()
    maps[me] = jnp.concatenate([slip[...].astype(jnp.float32), time[...]], axis=2)
    pl.semaphore_wait(barrier, sites + devices - 2)

    chunk = CHUNK
    chunks = tile_total // CHUNK

    def map_copy(part, step):
        tiles = pl.ds(part * chunk, chunk)
        return pltpu.make_async_remote_copy(
            src_ref=maps.at[me, tiles],
            dst_ref=maps.at[me, tiles],
            send_sem=map_send.at[part, step],
            recv_sem=map_recv.at[part, me],
            device_id={"site": lax.rem(me + step, sites)},
            device_id_type=MESH,
        )

    def map_arrival(part, step):
        source = lax.rem(me + step, sites)
        tiles = pl.ds(part * chunk, chunk)
        return pltpu.make_async_remote_copy(
            src_ref=maps.at[source, tiles],
            dst_ref=maps.at[source, tiles],
            send_sem=map_send.at[part, step],
            recv_sem=map_recv.at[part, source],
            device_id={"site": source},
            device_id_type=MESH,
        )

    def over(first, last, body):
        lax.fori_loop(first, last, lambda step, carry: (body(step), carry)[1], 0)

    over(0, chunks, lambda part: over(1, sites, lambda step: map_copy(part, step).start()))
    for tile in range(tile_total):
        pltpu.make_async_copy(green_hbm.at[tile], green.at[tile], green_sems.at[tile]).start()
    small[-1].start()
    for copy in small[2:-1]:
        copy.wait()
    member[...] = membership(ids, count, rupture, owner, rows, owner.shape[0])

    def arrive(part):
        over(1, sites, lambda step: map_arrival(part, step).wait_recv())

    def phasor_steps(tile, phasor):
        blocks = [maps[site, tile] for site in range(sites)]
        amplitude = jnp.concatenate([b[:, :local_points] for b in blocks], axis=1)
        arrival = jnp.concatenate([b[:, local_points:] for b in blocks], axis=1)
        return make_phasors(amplitude, arrival, freq_count, phasor)

    def dots_beside(tile, phasor, steps):
        block_count = freq_count // BLOCK
        share = -(-(2 * freq_count // (2 * HALF)) // block_count)
        for block in range(block_count):
            block_spectrum(tile, block, rows, green, phasor, spectrum)
            for _ in range(share):
                next(steps, None)
        for _ in steps:
            pass

    def green_arrive(tile):
        pltpu.make_async_copy(green_hbm.at[tile], green.at[tile], green_sems.at[tile]).wait()

    def pair(index):
        first = index * chunk
        arrive(index + 1)
        green_arrive(first)
        green_arrive(first + 1)
        dots_beside(first, phasors[0], phasor_steps(first + 1, phasors[1]))
        dots_beside(first + 1, phasors[1], phasor_steps(first + 2, phasors[0]))

    arrive(0)
    for _ in phasor_steps(0, phasors[0]):
        pass
    over(0, chunks - 1, pair)
    last = tile_total - 2
    green_arrive(last)
    green_arrive(last + 1)
    dots_beside(last, phasors[0], phasor_steps(last + 1, phasors[1]))
    dots_beside(last + 1, phasors[1], iter(()))
    routed = route_rows(member[...], spectrum[...])
    lanes = 4 * BLOCK
    routed = jnp.concatenate(
        [routed[:, at : at + 3 * BLOCK] for at in range(0, routed.shape[1], lanes)], axis=1
    )
    height = routed.shape[0] // devices
    for device in range(devices):
        partial[device] = routed[device * height : (device + 1) * height]

    def sum_copy(step):
        peer = lax.rem(mine + step, devices)
        return pltpu.make_async_remote_copy(
            src_ref=partial.at[peer],
            dst_ref=landed.at[mine],
            send_sem=sum_send.at[step],
            recv_sem=sum_recv.at[mine],
            device_id={"fault": peer},
            device_id_type=MESH,
        )

    def sum_arrival(step):
        source = lax.rem(mine + step, devices)
        return pltpu.make_async_remote_copy(
            src_ref=partial.at[source],
            dst_ref=landed.at[source],
            send_sem=sum_send.at[step],
            recv_sem=sum_recv.at[source],
            device_id={"fault": source},
            device_id_type=MESH,
        )

    over(1, devices, lambda step: sum_copy(step).start())
    small[-1].wait()
    total = partial[mine]
    for step in range(1, devices):
        sum_arrival(step).wait_recv()
        total = total + landed[lax.rem(mine + step, devices)]
    seismic = inverse(total, table[...], freq_count)
    for c in range(3):
        for row in range(height):
            at = c * height + row
            out[row, c] = seismic[at : at + 1]
    over(0, chunks, lambda part: over(1, sites, lambda step: map_copy(part, step).wait_send()))
    over(1, devices, lambda step: sum_copy(step).wait_send())


def per_device(
    sites, devices,
    green_tensor, slip_map, rupture_time, variation_ids, variation_count, tile_rupture, owner_slot,
):
    green = jnp.swapaxes(green_tensor[0], 1, 2)
    tile_total, _, freq_count, points = green.shape
    rows, local_points = slip_map.shape[1:]
    rupture_total = owner_slot.shape[0]
    width = 8 * freq_count
    height = rupture_total * rows // devices
    vmem = pl.BlockSpec(memory_space=pltpu.VMEM)
    anywhere = pl.BlockSpec(memory_space=pl.ANY)
    dma = pltpu.SemaphoreType.DMA
    seismic = pl.pallas_call(
        functools.partial(kernel, sites, devices),
        out_shape=jax.ShapeDtypeStruct((height, 3, 1, 2 * freq_count), jnp.float32),
        in_specs=[anywhere] * 8,
        out_specs=vmem,
        scratch_shapes=[
            pltpu.VMEM((rows, tile_total), jnp.int32),
            pltpu.SMEM((tile_total,), jnp.int32),
            pltpu.SMEM((tile_total,), jnp.int32),
            pltpu.SMEM((rupture_total,), jnp.int32),
            pltpu.VMEM(slip_map.shape, slip_map.dtype),
            pltpu.VMEM(rupture_time.shape, jnp.float32),
            pltpu.VMEM((2 * freq_count, 2 * freq_count), jnp.float32),
            pltpu.VMEM(green.shape, jnp.bfloat16),
            pltpu.VMEM((sites, tile_total, rows, 2 * local_points), jnp.float32),
            [pltpu.VMEM((freq_count * rows, 2 * points), jnp.bfloat16)] * 2,
            pltpu.VMEM((tile_total * 2 * rows, width), jnp.bfloat16),
            pltpu.VMEM((rupture_total * rows, tile_total * 2 * rows), jnp.bfloat16),
            pltpu.VMEM((devices, height, 6 * freq_count), jnp.float32),
            pltpu.VMEM((devices, height, 6 * freq_count), jnp.float32),
            dma((7,)),
            dma((tile_total,)),
            dma((tile_total // CHUNK, sites)),
            dma((tile_total // CHUNK, sites)),
            dma((devices,)),
            dma((devices,)),
        ],
        compiler_params=pltpu.CompilerParams(
            collective_id=0, has_side_effects=True, vmem_limit_bytes=60 * 1024 * 1024
        ),
        cost_estimate=pl.CostEstimate(flops=2 * 10**9, bytes_accessed=5 * 10**6, transcendentals=0),
    )(
        variation_ids.T, variation_count, tile_rupture, owner_slot,
        slip_map, rupture_time, inverse_table(freq_count), green,
    )
    seismic = seismic.reshape(rupture_total // devices, rows, 3, 1, 2 * freq_count)
    return jnp.swapaxes(seismic, 2, 3)


def solution(mesh):
    placed = (
        P("site", "fault", None, None, None),
        P("fault", None, "site"),
        P("fault", None, "site"),
        P("fault", None),
        P("fault"),
        P("fault"),
        P(),
    )
    return jax.shard_map(
        functools.partial(per_device, mesh.shape["site"], mesh.shape["fault"]),
        mesh=mesh,
        in_specs=placed,
        out_specs=P("fault", None, "site", None, None),
        check_vma=False,
    )
```
